512 devices in a mesh: dp: 64 (over x, z, core), head: 8 (over y).
Axes of the slice: x: 4, y: 8, z: 8, core: 2. Of those that a mesh axis runs over, the one named last changes fastest.
Arguments:
- projected: bfloat16 [8192, 7168], P(('dp', 'head')), may hold values from -64 to 64
- grad_output: bfloat16 [8192, 5120], P(('dp', 'head')), may hold values from -4 to 4
- prompt_cache: bfloat16 [32768, 2048], P('dp', 'head'), may hold values from -6 to 6
- segment_ids: int32 [64, 128], P('dp'), may hold values from 0 to 3, never falling along the last dimension, each value on 1 to 64 neighbouring positions
- segment_prompt: int32 [64, 4], P('dp'), may hold values from 0 to 63, as said below
Outputs:
- attention_out: bfloat16 [8192, 5120], P(('dp', 'head'))
- grad_projected: bfloat16 [8192, 7168], P(('dp', 'head'))
- grad_prompt_cache: bfloat16 [32768, 2048], P('dp', 'head')
The draws below stay inside these ranges and needn't reach their ends.
Inputs may be any that keep to these rules, and one draw needn't show every extreme that they name: `segment_ids`: on each index of dp the response numbers never fall, all 4 responses appear, each with 1 to 64 tokens. `segment_prompt`: the prompt of a response on dp index d is (d + o) mod 64 with o between -4 and 4; both ends occur.
All inputs are finite; a program needn't handle non-finite values.
Results may differ from the reference program's by a relative error of at most 0.04.
Values may be sent and summed in bfloat16 or wider, within the bound.
A program may use at most 64 MiB of HBM per device.

```python
import math
import jax
import jax.numpy as jnp
import numpy as np
from jax import lax

HEADS = 40
KV_HEADS = 8
HEAD_DIM = 128
TOK_DEV = 128
PROMPT_LEN = 512
SEGS = 4
REACH = 4
SEG_MOST = 64
PROMPTS = 64
TOKENS = 8192
N_DP = 64


def draw_projected(key, part):
    key = jax.random.fold_in(key, 5)
    group_size = HEADS // KV_HEADS
    shape = (TOKENS, KV_HEADS, group_size + 2, HEAD_DIM)
    base_key = jax.random.fold_in(key, 0)
    values = jax.random.truncated_normal(base_key, -6.0, 6.0, shape, jnp.float32)
    return values.reshape(TOKENS, KV_HEADS * (group_size + 2) * HEAD_DIM).astype(jnp.bfloat16)


def draw_segment_prompt(key, part):
    key = jax.random.fold_in(key, 11)
    distance = jax.random.randint(key, (PROMPTS, SEGS), -REACH, REACH + 1)
    distance = distance.at[0, 0].set(REACH).at[0, 1].set(0).at[0, SEGS - 1].set(-REACH).at[1, 0].set(-2)
    owner_rows = lax.iota(jnp.int32, PROMPTS)[:, None]
    return ((owner_rows + distance + PROMPTS) % PROMPTS).astype(jnp.int32)


def block_scale(key, shape, pieces, low, top_value):
    loudness = 1.0
    for axis_at, parts in pieces:
        heights = jax.random.uniform(jax.random.fold_in(jax.random.fold_in(key, 6), axis_at), (parts,), jnp.float32, low / len(pieces), top_value / len(pieces))
        loudness = loudness * jnp.repeat(jnp.exp(heights), shape[axis_at] // parts).reshape((-1,) + (1,) * (len(shape) - 1 - axis_at))
    return loudness


def split_up(count, total, bound, skew):
    portions = [(1 << 20) // math.isqrt(standing ** skew) + 1 for standing in range(2, count + 1)]
    rest, counts = total - bound - (count - 1), [1] * (count - 1)
    while rest > 0:
        candidates = [i for i in range(count - 1) if counts[i] < bound]
        pool, left = sum([portions[i] for i in candidates]), rest
        for i in candidates:
            more = min(bound - counts[i], max(1, left * portions[i] // pool), rest)
            counts[i] = counts[i] + more
            rest = rest - more
    return np.array([bound] + counts)


def ragged_sizes(own_key, amount, total, most, slope):
    if amount == 2:
        one = jax.random.randint(own_key, (), max(1, total - most), min(most, total - 1) + 1)
        return jnp.stack([one, total - one])
    lengths = jnp.asarray(split_up(amount, total, most, slope), jnp.int32)
    twos = (amount - 1) // 2
    giver, sink = lengths[1:1 + 2 * twos:2], lengths[2:2 + 2 * twos:2]
    slack = jnp.minimum(giver - 1, most - sink)
    passed = jax.random.randint(jax.random.fold_in(own_key, 1), (twos,), 0, 1 << 20) % (slack + 1)
    lengths = lengths.at[1:1 + 2 * twos:2].set(giver - passed).at[2:2 + 2 * twos:2].set(sink + passed)
    return lengths[jax.random.permutation(jax.random.fold_in(own_key, 2), amount)]


def gaussian(stream_key, extent, deviation, limit, pieces=(), held_as=jnp.bfloat16):
    gain = block_scale(stream_key, extent, pieces, -0.22, 0.18) if pieces else 1.0
    drawn = jax.random.normal(stream_key, extent, jnp.float32) * deviation * gain
    return jnp.minimum(jnp.maximum(drawn, -limit), limit).astype(held_as)


def setup_inputs(seed: int = 0) -> dict:
    arg_keys = jax.random.split(jax.random.key(seed), 6)
    projected = draw_projected(jax.random.fold_in(arg_keys[5], 71), 0)
    grad_output = gaussian(arg_keys[1], (TOKENS, HEADS * HEAD_DIM), 0.25, 4.0, ((0, 512),))
    prompt_cache = gaussian(arg_keys[2], (PROMPTS * PROMPT_LEN, KV_HEADS * 2 * HEAD_DIM), 1.0, 6.0, ((0, 64), (1, 8)))
    segment_ids = jax.vmap(lambda own: jnp.searchsorted(jnp.cumsum(ragged_sizes(own, SEGS, TOK_DEV, SEG_MOST, 2)), jnp.arange(TOK_DEV), side="right"))(jax.random.split(arg_keys[3], N_DP)).reshape((N_DP, TOK_DEV)).astype(jnp.int32)
    segment_prompt = draw_segment_prompt(jax.random.fold_in(arg_keys[5], 71), 0)
    return dict(projected=projected, grad_output=grad_output, prompt_cache=prompt_cache, segment_ids=segment_ids, segment_prompt=segment_prompt)


def product(form, left, right):
    return jnp.einsum(form, left.astype(jnp.float32), right.astype(jnp.float32))


def place(window, start, full_len, axis, fill):
    shape = list(window.shape)
    shape[axis] = full_len
    base = jnp.full(tuple(shape), fill, window.dtype)
    return lax.dynamic_update_slice_in_dim(base, window, start, axis)


def attend(queries, keys_now, values_now, dout, segment_row, prompt_blocks):
    row_count = queries.shape[0]
    width = SEG_MOST
    score_scale = queries.shape[-1] ** -0.5
    position = lax.iota(jnp.int32, row_count)
    self_mask = (segment_row[:, None] == segment_row[None, :]) & (position[None, :] <= position[:, None])
    self_scores = jnp.where(self_mask, product('tkgh,ukh->kgtu', queries, keys_now) * score_scale, -jnp.inf)
    prompt_keys = prompt_blocks[:, :, :, 0]
    prompt_values = prompt_blocks[:, :, :, 1]
    starts = []
    windows = []
    row_max = jnp.max(self_scores, axis=-1)
    for segment in range(SEGS):
        first = jnp.sum((segment_row < segment).astype(jnp.int32))
        start = jnp.clip(first, 0, row_count - width).astype(jnp.int32)
        live = lax.dynamic_slice_in_dim(segment_row, start, width, 0) == segment
        query_win = lax.dynamic_slice_in_dim(queries, start, width, 0)
        scores = jnp.where(live[None, None, :, None], product('tkgh,lkh->kgtl', query_win, prompt_keys[segment]) * score_scale, -jnp.inf)
        row_max = jnp.maximum(row_max, place(jnp.max(scores, axis=-1), start, row_count, 2, -jnp.inf))
        starts.append(start)
        windows.append(scores)
    self_exp = jnp.exp(self_scores - row_max[..., None])
    row_total = jnp.sum(self_exp, axis=-1)
    exps = []
    for segment in range(SEGS):
        start = starts[segment]
        max_win = lax.dynamic_slice_in_dim(row_max, start, width, 2)
        expo = jnp.exp(windows[segment] - max_win[..., None])
        row_total = row_total + place(jnp.sum(expo, axis=-1), start, row_count, 2, 0.0)
        exps.append(expo)
    self_weight = self_exp / row_total[..., None]
    self_rounded = self_weight.astype(jnp.bfloat16)
    attended = product('kgtu,ukh->tkgh', self_rounded, values_now)
    weights = []
    for segment in range(SEGS):
        start = starts[segment]
        total_win = lax.dynamic_slice_in_dim(row_total, start, width, 2)
        weight = exps[segment] / total_win[..., None]
        rounded = weight.astype(jnp.bfloat16)
        attended = attended + place(product('kgtl,lkh->tkgh', rounded, prompt_values[segment]), start, row_count, 0, 0.0)
        weights.append((weight, rounded))
    attended = attended.astype(jnp.bfloat16)
    dot_term = jnp.sum(dout.astype(jnp.float32) * attended.astype(jnp.float32), axis=-1)
    delta = jnp.transpose(dot_term, (1, 2, 0))
    self_grad = (self_weight * (product('tkgh,ukh->kgtu', dout, values_now) - delta[..., None]) * score_scale).astype(jnp.bfloat16)
    query_grad = product('kgtu,ukh->tkgh', self_grad, keys_now)
    prompt_terms = []
    for segment in range(SEGS):
        start = starts[segment]
        weight, rounded = weights[segment]
        dout_win = lax.dynamic_slice_in_dim(dout, start, width, 0)
        query_win = lax.dynamic_slice_in_dim(queries, start, width, 0)
        delta_win = lax.dynamic_slice_in_dim(delta, start, width, 2)
        prefix_grad = (weight * (product('tkgh,lkh->kgtl', dout_win, prompt_values[segment]) - delta_win[..., None]) * score_scale).astype(jnp.bfloat16)
        query_grad = query_grad + place(product('kgtl,lkh->tkgh', prefix_grad, prompt_keys[segment]), start, row_count, 0, 0.0)
        prompt_dkey = product('kgtl,tkgh->lkh', prefix_grad, query_win)
        prompt_dvalue = product('kgtl,tkgh->lkh', rounded, dout_win)
        prompt_terms.append(jnp.stack([prompt_dkey, prompt_dvalue], axis=2))
    d_query = query_grad.astype(jnp.bfloat16)
    d_key = product('kgtu,tkgh->ukh', self_grad, queries).astype(jnp.bfloat16)
    d_value = product('kgtu,tkgh->ukh', self_rounded, dout).astype(jnp.bfloat16)
    d_packed = jnp.concatenate([d_query, d_key[:, :, None], d_value[:, :, None]], axis=2)
    return attended, d_packed, jnp.stack(prompt_terms, axis=0)


def reference(projected, grad_output, prompt_cache, segment_ids, segment_prompt):
    group_size = HEADS // KV_HEADS
    packed = projected.reshape(N_DP, TOK_DEV, KV_HEADS, group_size + 2, HEAD_DIM)
    douts = grad_output.reshape(N_DP, TOK_DEV, KV_HEADS, group_size, HEAD_DIM)
    prompts = prompt_cache.reshape(PROMPTS, PROMPT_LEN, KV_HEADS, 2, HEAD_DIM)

    def visit(carried, item):
        packed_row, dout_row, segment_row, owners = item
        blocks = prompts[owners]
        attended, d_packed, prompt_terms = attend(packed_row[:, :, :group_size], packed_row[:, :, group_size], packed_row[:, :, group_size + 1], dout_row, segment_row, blocks)
        carried = carried.at[owners].add(prompt_terms)
        return carried, (attended, d_packed)

    start = jnp.zeros((PROMPTS, PROMPT_LEN, KV_HEADS, 2, HEAD_DIM), jnp.float32)
    summed, (attended, d_packed) = lax.scan(visit, start, (packed, douts, segment_ids, segment_prompt))
    attention_out = attended.reshape(TOKENS, HEADS * HEAD_DIM)
    grad_projected = d_packed.reshape(TOKENS, KV_HEADS * (group_size + 2) * HEAD_DIM)
    grad_prompt_cache = summed.reshape(PROMPTS * PROMPT_LEN, KV_HEADS * 2 * HEAD_DIM).astype(jnp.bfloat16)
    return attention_out, grad_projected, grad_prompt_cache
```

```python
import jax
import jax.numpy as jnp
from jax import lax
from jax.experimental import pallas as pl
from jax.experimental.pallas import tpu as pltpu
from jax.sharding import PartitionSpec as P

HEADS = 40
KV_HEADS = 8
HEAD_DIM = 128
GROUP = HEADS // KV_HEADS
TOK_DEV = 128
PROMPT_LEN = 512
SEGS = 4
REACH = 4
SEG_MOST = 64
N_DP = 64
CHIPS = N_DP // 2
N_HEAD = 8
ROWS = TOK_DEV // N_HEAD
PACK = (GROUP + 2) * HEAD_DIM
OUT = GROUP * HEAD_DIM
STACK = GROUP * SEG_MOST
KEYS = PROMPT_LEN + HEAD_DIM
SCALE = HEAD_DIM**-0.5
LOG2E = 1.4426950408889634
MESH = pl.DeviceIdType.MESH
F32 = jnp.float32
BF16 = jnp.bfloat16
COPIES = 72


def dot(left, right, contract):
    return lax.dot_general(left, right, (contract, ((), ())), preferred_element_type=F32)


def heads_down(block):
    return jnp.concatenate([block[:, g * HEAD_DIM : (g + 1) * HEAD_DIM] for g in range(GROUP)], axis=0)


def kernel(
    ids_ref, owner_ref, proj, gout, cache,
    att_out, dproj_out, dcache_out,
    pk, dk, keys, values, win_q, win_kv, win_d, prob, term, win_o, win_g, att_send, dproj_send,
    sib_send, sib_recv, far_send, far_recv, near_send, near_recv,
    local_sem, send_sem, recv_sem,
):
    dp = lax.axis_index("dp")
    head = lax.axis_index("head")
    chip = dp // 2
    core = lax.rem(dp, 2)
    sibling = (dp + 1 - 2 * core, head)
    right = (lax.rem(chip + 1, CHIPS) * 2 + core, head)
    left = (lax.rem(chip + CHIPS - 1, CHIPS) * 2 + core, head)
    peers = [lax.rem(head + j, N_HEAD) for j in range(1, N_HEAD)]
    used = [0]
    kv = (keys, values)

    def send(src, dst, device):
        i = used[0]
        used[0] += 1
        copy = pltpu.make_async_remote_copy(
            src_ref=src, dst_ref=dst, send_sem=send_sem.at[i], recv_sem=recv_sem.at[i],
            device_id=device, device_id_type=MESH,
        )
        copy.start()
        return copy

    def columns(index, width):
        return pl.ds(pl.multiple_of(index * width, HEAD_DIM), width)

    local = [
        pltpu.make_async_copy(cache.at[:, pl.ds(w * HEAD_DIM, HEAD_DIM)], kv[w].at[2], local_sem.at[w])
        for w in range(2)
    ]
    local.append(pltpu.make_async_copy(proj.at[:, columns(head, PACK)], pk.at[head], local_sem.at[2]))
    local.append(pltpu.make_async_copy(gout.at[:, columns(head, OUT)], dk.at[head], local_sem.at[3]))
    for copy in local:
        copy.start()
    barrier = pltpu.get_barrier_semaphore()
    partners = [sibling, right, left] + [(dp, p) for p in peers]
    for partner in partners:
        pl.semaphore_signal(barrier, inc=1, device_id=partner, device_id_type=MESH)

    ids = ids_ref[...]
    position = lax.broadcasted_iota(jnp.int32, (1, TOK_DEV), 1)
    first = jnp.zeros((1, TOK_DEV), jnp.int32)
    for s in range(SEGS):
        before = jnp.sum((ids < s).astype(jnp.int32), axis=1, keepdims=True)
        first = first + jnp.where(ids == s, before, 0)
    row = (ids * SEG_MOST + position - first).astype(F32)
    rows = lax.broadcasted_iota(jnp.int32, (SEGS * SEG_MOST, TOK_DEV), 0).astype(F32)
    pick = (jnp.broadcast_to(row, rows.shape) == rows).astype(BF16)
    row_t = jnp.transpose(jnp.broadcast_to(row, (TOK_DEV, TOK_DEV)))
    cols = lax.broadcasted_iota(jnp.int32, (TOK_DEV, SEGS * SEG_MOST), 1).astype(F32)
    unpick = (jnp.concatenate([row_t, row_t], axis=1) == cols).astype(BF16)

    offsets, slots = [], []
    for s in range(SEGS):
        offset = lax.rem(owner_ref[0, s] - dp + N_DP + REACH, N_DP) - REACH
        odd = lax.rem(offset + 8, 2)
        away = jnp.where(odd == 1, offset - 1 + 2 * core, offset) // 2
        slot = jnp.where(
            odd == 0, jnp.clip(away, -2, 2) + 2,
            jnp.where(away == 0, 5, jnp.where(away == 1, 6, jnp.where(away == -1, 7, 8))),
        )
        offsets.append(offset)
        slots.append(slot)

    def slot_of(s):
        return jnp.where(s == 0, slots[0], jnp.where(s == 1, slots[1], jnp.where(s == 2, slots[2], slots[3])))

    for w in range(2):
        local[w].wait()
    pl.semaphore_wait(barrier, len(partners))

    pending = []
    near, far, sib = [None, None], [None, None], [[], []]
    a2a = [[], []]
    near[0] = [send(kv[0].at[2], kv[0].at[1], right), send(kv[0].at[2], kv[0].at[3], left)]
    sib[0].append(send(kv[0].at[2], kv[0].at[5], sibling))
    for p in peers:
        a2a[0].append(send(proj.at[:, columns(p, PACK)], pk.at[head], (dp, p)))
    near[1] = [send(kv[1].at[2], kv[1].at[1], right), send(kv[1].at[2], kv[1].at[3], left)]
    sib[1].append(send(kv[1].at[2], kv[1].at[5], sibling))
    for p in peers:
        a2a[1].append(send(gout.at[:, columns(p, OUT)], dk.at[head], (dp, p)))
    for w in range(2):
        near[w][0].wait_recv()
        f0 = send(kv[w].at[1], kv[w].at[0], right)
        sib[w].append(send(kv[w].at[1], kv[w].at[7], sibling))
        near[w][1].wait_recv()
        f1 = send(kv[w].at[3], kv[w].at[4], left)
        sib[w].append(send(kv[w].at[3], kv[w].at[6], sibling))
        far[w] = [f0, f1]

    def spread(picked, window):
        for g in range(GROUP):
            part = picked[:, g * HEAD_DIM : (g + 1) * HEAD_DIM]
            window[:, g] = part.reshape(SEGS, SEG_MOST, HEAD_DIM)

    local[2].wait()
    local[3].wait()
    for copy in a2a[0]:
        copy.wait_recv()
    picked = dot(pick, pk[...].reshape(TOK_DEV, PACK), ((1,), (0,))).astype(BF16)
    spread(picked, win_q)
    for w in range(2):
        own = picked[:, OUT + w * HEAD_DIM : OUT + (w + 1) * HEAD_DIM].reshape(SEGS, SEG_MOST, HEAD_DIM)
        win_kv[w] = jnp.concatenate([own, jnp.zeros_like(own)], axis=1)
    for copy in a2a[1]:
        copy.wait_recv()
    picked = dot(pick, dk[...].reshape(TOK_DEV, OUT), ((1,), (0,))).astype(BF16)
    spread(picked, win_d)

    def arrived(w):
        for copy in far[w]:
            copy.wait_recv()
        sib[w].append(send(kv[w].at[4 - 4 * core], kv[w].at[8], sibling))
        for copy in sib[w]:
            copy.wait_recv()

    def all_rows(w, s):
        return jnp.concatenate([kv[w][slot_of(s)], win_kv[w, s]], axis=0)

    key_at = lax.broadcasted_iota(jnp.int32, (STACK, HEAD_DIM), 1)
    row_at = lax.rem(lax.broadcasted_iota(jnp.int32, (STACK, HEAD_DIM), 0), SEG_MOST)

    def weigh(s, carry):
        queries = win_q[s].reshape(STACK, HEAD_DIM)
        dout = win_d[s].reshape(STACK, HEAD_DIM)
        scores = dot(queries, all_rows(0, s), ((1,), (1,)))
        own = jnp.where(key_at <= row_at, scores[:, PROMPT_LEN:], -1e30)
        scores = jnp.concatenate([scores[:, :PROMPT_LEN], own], axis=1)
        top = jnp.max(scores, axis=1, keepdims=True)
        expo = jnp.exp2((scores - top) * (SCALE * LOG2E))
        weights = expo * (1.0 / jnp.sum(expo, axis=1, keepdims=True))
        prob[s] = weights
        dvalue = dot(weights.astype(BF16), dout, ((0,), (0,)))
        term[1, s] = dvalue[:PROMPT_LEN]
        win_g[s, GROUP + 1] = dvalue[PROMPT_LEN : PROMPT_LEN + SEG_MOST].astype(BF16)
        return carry

    def attend(s, carry):
        out = dot(prob[s].astype(BF16), all_rows(1, s), ((1,), (0,))).astype(BF16)
        win_o[s] = out.reshape(GROUP, SEG_MOST, HEAD_DIM)
        return carry

    def differentiate(s, carry):
        queries = win_q[s].reshape(STACK, HEAD_DIM)
        dout = win_d[s].reshape(STACK, HEAD_DIM)
        out = win_o[s].reshape(STACK, HEAD_DIM)
        delta = jnp.sum(dout.astype(F32) * out.astype(F32), axis=1, keepdims=True)
        dweight = dot(dout, all_rows(1, s), ((1,), (1,)))
        dscore = (prob[s] * (dweight - delta) * SCALE).astype(BF16)
        dquery = dot(dscore, all_rows(0, s), ((1,), (0,))).astype(BF16)
        win_g[s, :GROUP] = dquery.reshape(GROUP, SEG_MOST, HEAD_DIM)
        dkey = dot(dscore, queries, ((0,), (0,)))
        term[0, s] = dkey[:PROMPT_LEN]
        win_g[s, GROUP] = dkey[PROMPT_LEN : PROMPT_LEN + SEG_MOST].astype(BF16)
        return carry

    def summed(w, offset):
        total = jnp.zeros((PROMPT_LEN, HEAD_DIM), F32)
        for s in range(SEGS):
            total = total + jnp.where(offsets[s] == offset, term[w, s], 0.0)
        return total

    def to_sibling(w):
        copies = []
        for i, away in enumerate((-1, 0, 1)):
            sib_send[w, i] = summed(w, 2 * away + 1 - 2 * core).astype(BF16)
        sib_send[w, 3] = summed(w, 6 * core - 3).astype(BF16)
        for i in (3, 0, 2, 1):
            copies.append(send(sib_send.at[w, i], sib_recv.at[w, i], sibling))
        return copies

    def to_far(w, copies):
        for copy in copies:
            copy.wait_recv()
        extra = sib_recv[w, 3].astype(F32)
        far_send[w, 0] = (summed(w, 4) + jnp.where(core == 0, extra, 0.0)).astype(BF16)
        far_send[w, 1] = (summed(w, -4) + jnp.where(core == 1, extra, 0.0)).astype(BF16)
        return [
            send(far_send.at[w, 0], far_recv.at[w, 0], right),
            send(far_send.at[w, 1], far_recv.at[w, 1], left),
        ]

    def to_near(w, copies):
        sent = []
        for i, device in enumerate((right, left)):
            copies[i].wait_recv()
            part = summed(w, 2 - 4 * i) + sib_recv[w, 2 - 2 * i].astype(F32) + far_recv[w, i].astype(F32)
            near_send[w, i] = part.astype(BF16)
            sent.append(send(near_send.at[w, i], near_recv.at[w, i], device))
        return sent

    def finish(w, copies):
        total = summed(w, 0) + sib_recv[w, 1].astype(F32)
        for i in range(2):
            copies[i].wait_recv()
            total = total + near_recv[w, i].astype(F32)
        dcache_out[:, w * HEAD_DIM : (w + 1) * HEAD_DIM] = total.astype(BF16)

    def give_back(window, staged, out, width, sem):
        parts = [window[:, g].reshape(SEGS * SEG_MOST, HEAD_DIM) for g in range(width // HEAD_DIM)]
        tokens = dot(unpick, jnp.concatenate(parts, axis=1), ((1,), (0,)))
        staged[...] = tokens.astype(BF16).reshape(N_HEAD, ROWS, width)
        copies = [send(staged.at[p], out.at[:, columns(head, width)], (dp, p)) for p in peers]
        own = pltpu.make_async_copy(staged.at[head], out.at[:, columns(head, width)], local_sem.at[sem])
        own.start()
        return copies, own

    arrived(0)
    lax.fori_loop(0, SEGS, weigh, 0)
    value_sib = to_sibling(1)
    arrived(1)
    value_far = to_far(1, value_sib)
    lax.fori_loop(0, SEGS, attend, 0)
    att_copies, att_own = give_back(win_o, att_send, att_out, OUT, 0)
    lax.fori_loop(0, SEGS, differentiate, 0)
    grad_copies, grad_own = give_back(win_g, dproj_send, dproj_out, PACK, 1)
    key_sib = to_sibling(0)
    value_near = to_near(1, value_far)
    key_far = to_far(0, key_sib)
    finish(1, value_near)
    key_near = to_near(0, key_far)
    finish(0, key_near)
    for copy in att_copies + grad_copies:
        copy.wait_recv()
    att_own.wait()
    grad_own.wait()
    sent = near[0] + near[1] + far[0] + far[1] + sib[0] + sib[1] + a2a[0] + a2a[1]
    sent += value_sib + value_far + value_near + key_sib + key_far + key_near + att_copies + grad_copies
    assert len(sent) == used[0] <= COPIES
    for copy in sent:
        copy.wait_send()


def local(projected, grad_output, prompt_cache, segment_ids, segment_prompt):
    hbm = pl.BlockSpec(memory_space=pl.ANY)
    vmem = pl.BlockSpec(memory_space=pltpu.VMEM)
    smem = pl.BlockSpec(memory_space=pltpu.SMEM)
    block = (PROMPT_LEN, HEAD_DIM)
    return pl.pallas_call(
        kernel,
        out_shape=(
            jax.ShapeDtypeStruct(grad_output.shape, BF16),
            jax.ShapeDtypeStruct(projected.shape, BF16),
            jax.ShapeDtypeStruct(prompt_cache.shape, BF16),
        ),
        in_specs=[vmem, smem, hbm, hbm, hbm],
        out_specs=(hbm, hbm, vmem),
        scratch_shapes=[
            pltpu.VMEM((N_HEAD, ROWS, PACK), BF16),
            pltpu.VMEM((N_HEAD, ROWS, OUT), BF16),
            pltpu.VMEM((9,) + block, BF16),
            pltpu.VMEM((9,) + block, BF16),
            pltpu.VMEM((SEGS, GROUP, SEG_MOST, HEAD_DIM), BF16),
            pltpu.VMEM((2, SEGS, HEAD_DIM, HEAD_DIM), BF16),
            pltpu.VMEM((SEGS, GROUP, SEG_MOST, HEAD_DIM), BF16),
            pltpu.VMEM((SEGS, STACK, KEYS), F32),
            pltpu.VMEM((2, SEGS) + block, F32),
            pltpu.VMEM((SEGS, GROUP, SEG_MOST, HEAD_DIM), BF16),
            pltpu.VMEM((SEGS, GROUP + 2, SEG_MOST, HEAD_DIM), BF16),
            pltpu.VMEM((N_HEAD, ROWS, OUT), BF16),
            pltpu.VMEM((N_HEAD, ROWS, PACK), BF16),
            pltpu.VMEM((2, 4) + block, BF16),
            pltpu.VMEM((2, 4) + block, BF16),
            pltpu.VMEM((2, 2) + block, BF16),
            pltpu.VMEM((2, 2) + block, BF16),
            pltpu.VMEM((2, 2) + block, BF16),
            pltpu.VMEM((2, 2) + block, BF16),
            pltpu.SemaphoreType.DMA((4,)),
            pltpu.SemaphoreType.DMA((COPIES,)),
            pltpu.SemaphoreType.DMA((COPIES,)),
        ],
        compiler_params=pltpu.CompilerParams(
            collective_id=0, has_side_effects=True, vmem_limit_bytes=62 << 20
        ),
    )(segment_ids, segment_prompt, projected, grad_output, prompt_cache)


def solution(mesh):
    return jax.shard_map(
        local,
        mesh=mesh,
        in_specs=(
            P(("dp", "head"), None),
            P(("dp", "head"), None),
            P("dp", "head"),
            P("dp", None),
            P("dp", None),
        ),
        out_specs=(P(("dp", "head"), None), P(("dp", "head"), None), P("dp", "head")),
        check_vma=False,
    )
```

```python
import jax
import jax.numpy as jnp
from jax import lax
from jax.experimental import pallas as pl
from jax.experimental.pallas import tpu as pltpu
from jax.sharding import PartitionSpec as P

HEADS = 40
KV_HEADS = 8
HEAD_DIM = 128
GROUP = HEADS // KV_HEADS
TOK_DEV = 128
PROMPT_LEN = 512
SEGS = 4
REACH = 4
SEG_MOST = 64
N_DP = 64
CHIPS = N_DP // 2
N_HEAD = 8
ROWS = TOK_DEV // N_HEAD
PACK = (GROUP + 2) * HEAD_DIM
OUT = GROUP * HEAD_DIM
STACK = GROUP * SEG_MOST
KEYS = PROMPT_LEN + HEAD_DIM
SCALE = HEAD_DIM**-0.5
LOG2E = 1.4426950408889634
MESH = pl.DeviceIdType.MESH
F32 = jnp.float32
BF16 = jnp.bfloat16
COPIES = 80
HALF = PROMPT_LEN // 2


def dot(left, right, contract):
    return lax.dot_general(left, right, (contract, ((), ())), preferred_element_type=F32)


def kernel(
    ids_ref, owner_ref, proj, gout, cache,
    att_out, dproj_out, dcache_out,
    pk, dk, keys, values, win_q, win_kv, win_d, prob, prob_b, dscore_b, term, win_o, win_g, att_send, dproj_send,
    sib_send, sib_recv, far_send, far_recv, near_send, near_recv,
    local_sem, send_sem, recv_sem,
):
    dp = lax.axis_index("dp")
    head = lax.axis_index("head")
    chip = dp // 2
    core = lax.rem(dp, 2)
    sibling = (dp + 1 - 2 * core, head)
    right = (lax.rem(chip + 1, CHIPS) * 2 + core, head)
    left = (lax.rem(chip + CHIPS - 1, CHIPS) * 2 + core, head)
    peers = [lax.rem(head + j, N_HEAD) for j in range(1, N_HEAD)]
    kv = (keys, values)
    sent = []

    def send(src, dst, device):
        i = len(sent)
        copy = pltpu.make_async_remote_copy(
            src_ref=src, dst_ref=dst, send_sem=send_sem.at[i], recv_sem=recv_sem.at[i],
            device_id=device, device_id_type=MESH,
        )
        copy.start()
        sent.append(copy)
        return copy

    def columns(index, width):
        return pl.ds(pl.multiple_of(index * width, HEAD_DIM), width)

    def feature(w):
        return pl.ds(w * HEAD_DIM, HEAD_DIM)

    halves = [pl.ds(i * HALF, HALF) for i in range(2)]

    own_kv = [pltpu.make_async_copy(cache.at[:, feature(w)], kv[w].at[2], local_sem.at[w]) for w in range(2)]
    own_proj = pltpu.make_async_copy(proj.at[:, columns(head, PACK)], pk.at[head], local_sem.at[2])
    own_gout = pltpu.make_async_copy(gout.at[:, columns(head, OUT)], dk.at[head], local_sem.at[3])
    for copy in own_kv + [own_proj, own_gout]:
        copy.start()
    barrier = pltpu.get_barrier_semaphore()
    partners = [right, left, sibling] + [(dp, p) for p in peers]
    for partner in partners:
        pl.semaphore_signal(barrier, inc=1, device_id=partner, device_id_type=MESH)

    ids = ids_ref[...]
    position = lax.broadcasted_iota(jnp.int32, (1, TOK_DEV), 1)
    first = jnp.zeros((1, TOK_DEV), jnp.int32)
    for s in range(SEGS):
        before = jnp.sum((ids < s).astype(jnp.int32), axis=1, keepdims=True)
        first = first + jnp.where(ids == s, before, 0)
    row = (ids * SEG_MOST + position - first).astype(F32)
    rows = lax.broadcasted_iota(jnp.int32, (SEGS * SEG_MOST, TOK_DEV), 0).astype(F32)
    pick = (jnp.broadcast_to(row, rows.shape) == rows).astype(BF16)
    row_t = jnp.transpose(jnp.broadcast_to(row, (TOK_DEV, TOK_DEV)))
    cols = lax.broadcasted_iota(jnp.int32, (TOK_DEV, SEGS * SEG_MOST), 1).astype(F32)
    unpick = (jnp.concatenate([row_t, row_t], axis=1) == cols).astype(BF16)

    offsets, slots = [], []
    for s in range(SEGS):
        offset = lax.rem(owner_ref[0, s] - dp + N_DP + REACH, N_DP) - REACH
        odd = lax.rem(offset + 8, 2)
        away = jnp.where(odd == 1, offset - 1 + 2 * core, offset) // 2
        slot = jnp.where(
            odd == 0, jnp.clip(away, -2, 2) + 2,
            jnp.where(away == 0, 5, jnp.where(away == 1, 6, jnp.where(away == -1, 7, 8))),
        )
        offsets.append(offset)
        slots.append(slot)

    pl.semaphore_wait(barrier, len(partners))

    def start_near(w):
        copies = []
        for half in halves:
            block = cache.at[half, feature(w)]
            copies.append(send(block, kv[w].at[1, half], right))
            copies.append(send(block, kv[w].at[3, half], left))
        return copies

    def relay(w, i, near):
        near[2 * i].wait_recv()
        from_left = send(kv[w].at[1, halves[i]], kv[w].at[0, halves[i]], right)
        near[2 * i + 1].wait_recv()
        from_right = send(kv[w].at[3, halves[i]], kv[w].at[4, halves[i]], left)
        return [from_left, from_right]

    def share_near(w):
        return [send(kv[w].at[1], kv[w].at[7], sibling), send(kv[w].at[3], kv[w].at[6], sibling)]

    def share_far(w, far):
        for copy in far:
            copy.wait_recv()
        return [send(kv[w].at[4 - 4 * core], kv[w].at[8], sibling)]

    near_k = start_near(0)
    sib_k = [send(cache.at[:, feature(0)], keys.at[5], sibling)]
    a2a_p = [send(proj.at[:, columns(p, PACK)], pk.at[head], (dp, p)) for p in peers]
    far_k = relay(0, 0, near_k)
    far_k += relay(0, 1, near_k)
    near_v = start_near(1)
    sib_k += share_near(0)
    a2a_g = [send(gout.at[:, columns(p, OUT)], dk.at[head], (dp, p)) for p in peers]
    sib_v = [send(cache.at[:, feature(1)], values.at[5], sibling)]

    def spread(picked, window):
        for g in range(GROUP):
            part = picked[:, g * HEAD_DIM : (g + 1) * HEAD_DIM]
            window[:, g] = part.reshape(SEGS, SEG_MOST, HEAD_DIM)

    def gather_proj():
        own_proj.wait()
        for copy in a2a_p:
            copy.wait_recv()
        picked = dot(pick, pk[...].reshape(TOK_DEV, PACK), ((1,), (0,))).astype(BF16)
        spread(picked, win_q)
        for w in range(2):
            own = picked[:, OUT + w * HEAD_DIM : OUT + (w + 1) * HEAD_DIM].reshape(SEGS, SEG_MOST, HEAD_DIM)
            win_kv[w] = jnp.concatenate([own, jnp.zeros_like(own)], axis=1)

    def gather_gout():
        own_gout.wait()
        for copy in a2a_g:
            copy.wait_recv()
        spread(dot(pick, dk[...].reshape(TOK_DEV, OUT), ((1,), (0,))).astype(BF16), win_d)

    def all_rows(w, s):
        return jnp.concatenate([kv[w][slots[s]], win_kv[w, s]], axis=0)

    def queries(s):
        return win_q[s].reshape(STACK, HEAD_DIM)

    def dout(s):
        return win_d[s].reshape(STACK, HEAD_DIM)

    key_at = lax.broadcasted_iota(jnp.int32, (STACK, HEAD_DIM), 1)
    row_at = lax.rem(lax.broadcasted_iota(jnp.int32, (STACK, HEAD_DIM), 0), SEG_MOST)

    def weigh(s):
        scores = dot(queries(s), all_rows(0, s), ((1,), (1,)))
        own = jnp.where(key_at <= row_at, scores[:, PROMPT_LEN:], -1e30)
        scores = jnp.concatenate([scores[:, :PROMPT_LEN], own], axis=1)
        top = jnp.max(scores, axis=1, keepdims=True)
        expo = jnp.exp2((scores - top) * (SCALE * LOG2E))
        weights = expo * (1.0 / jnp.sum(expo, axis=1, keepdims=True))
        prob[s] = weights
        prob_b[s] = weights.astype(BF16)

    def value_terms(s):
        dvalue = dot(prob_b[s], dout(s), ((0,), (0,)))
        term[1, s] = dvalue[:PROMPT_LEN]
        win_g[s, GROUP + 1] = dvalue[PROMPT_LEN : PROMPT_LEN + SEG_MOST].astype(BF16)

    def attend(s):
        out = dot(prob_b[s], all_rows(1, s), ((1,), (0,))).astype(BF16)
        win_o[s] = out.reshape(GROUP, SEG_MOST, HEAD_DIM)

    def key_terms(s):
        out = win_o[s].reshape(STACK, HEAD_DIM)
        delta = jnp.sum(dout(s).astype(F32) * out.astype(F32), axis=1, keepdims=True)
        dweight = dot(dout(s), all_rows(1, s), ((1,), (1,)))
        dscore = (prob[s] * (dweight - delta) * SCALE).astype(BF16)
        dscore_b[s] = dscore
        dkey = dot(dscore, queries(s), ((0,), (0,)))
        term[0, s] = dkey[:PROMPT_LEN]
        win_g[s, GROUP] = dkey[PROMPT_LEN : PROMPT_LEN + SEG_MOST].astype(BF16)

    def query_terms(s):
        dquery = dot(dscore_b[s], all_rows(0, s), ((1,), (0,))).astype(BF16)
        win_g[s, :GROUP] = dquery.reshape(GROUP, SEG_MOST, HEAD_DIM)

    def summed(w, offset, part):
        total = jnp.zeros((part.size, HEAD_DIM), F32)
        for s in range(SEGS):
            total = total + jnp.where(offsets[s] == offset, term[w, s, part], 0.0)
        return total

    whole = pl.ds(0, PROMPT_LEN)

    def to_sibling(w):
        copies = [None] * 4
        for i, offset in ((3, 6 * core - 3), (0, -1 - 2 * core), (2, 3 - 2 * core), (1, 1 - 2 * core)):
            sib_send[w, i] = summed(w, offset, whole).astype(BF16)
            copies[i] = send(sib_send.at[w, i], sib_recv.at[w, i], sibling)
        return copies

    def to_far(w, sib):
        sib[3].wait_recv()
        copies = []
        for half in halves:
            extra = sib_recv[w, 3, half].astype(F32)
            far_send[w, 0, half] = (summed(w, 4, half) + jnp.where(core == 0, extra, 0.0)).astype(BF16)
            copies.append(send(far_send.at[w, 0, half], far_recv.at[w, 0, half], right))
            far_send[w, 1, half] = (summed(w, -4, half) + jnp.where(core == 1, extra, 0.0)).astype(BF16)
            copies.append(send(far_send.at[w, 1, half], far_recv.at[w, 1, half], left))
        return copies

    def to_near(w, h, sib, far):
        half = halves[h]
        copies = []
        for i, device in enumerate((right, left)):
            if h == 0:
                sib[2 - 2 * i].wait_recv()
            part = summed(w, 2 - 4 * i, half) + sib_recv[w, 2 - 2 * i, half].astype(F32)
            far[2 * h + i].wait_recv()
            near_send[w, i, half] = (part + far_recv[w, i, half].astype(F32)).astype(BF16)
            copies.append(send(near_send.at[w, i, half], near_recv.at[w, i, half], device))
        return copies

    def finish(w, h, sib, near):
        half = halves[h]
        if h == 0:
            sib[1].wait_recv()
        total = summed(w, 0, half) + sib_recv[w, 1, half].astype(F32)
        for i in range(2):
            near[2 * h + i].wait_recv()
            total = total + near_recv[w, i, half].astype(F32)
        dcache_out[half, feature(w)] = total.astype(BF16)

    def give_back(window, staged, out, width, sem):
        parts = [window[:, g].reshape(SEGS * SEG_MOST, HEAD_DIM) for g in range(width // HEAD_DIM)]
        tokens = dot(unpick, jnp.concatenate(parts, axis=1), ((1,), (0,)))
        staged[...] = tokens.astype(BF16).reshape(N_HEAD, ROWS, width)
        copies = [send(staged.at[p], out.at[:, columns(head, width)], (dp, p)) for p in peers]
        own = pltpu.make_async_copy(staged.at[head], out.at[:, columns(head, width)], local_sem.at[sem])
        own.start()
        return copies, own

    gather_proj()
    sib_k += share_far(0, far_k)
    own_kv[0].wait()
    for copy in sib_k:
        copy.wait_recv()
    weigh(0)
    far_v = relay(1, 0, near_v)
    weigh(1)
    far_v += relay(1, 1, near_v)
    sib_v += share_near(1)
    weigh(2)
    weigh(3)
    gather_gout()
    for s in range(SEGS):
        value_terms(s)
    value_sib = to_sibling(1)
    sib_v += share_far(1, far_v)
    value_far = to_far(1, value_sib)
    own_kv[1].wait()
    for copy in sib_v:
        copy.wait_recv()
    for s in range(SEGS):
        attend(s)
    att_copies, att_own = give_back(win_o, att_send, att_out, OUT, 0)
    key_terms(0)
    key_terms(1)
    value_near = to_near(1, 0, value_sib, value_far)
    key_terms(2)
    key_terms(3)
    key_sib = to_sibling(0)
    value_near += to_near(1, 1, value_sib, value_far)
    for s in range(SEGS):
        query_terms(s)
    key_far = to_far(0, key_sib)
    grad_copies, grad_own = give_back(win_g, dproj_send, dproj_out, PACK, 1)
    finish(1, 0, value_sib, value_near)
    finish(1, 1, value_sib, value_near)
    key_near = to_near(0, 0, key_sib, key_far)
    key_near += to_near(0, 1, key_sib, key_far)
    finish(0, 0, key_sib, key_near)
    finish(0, 1, key_sib, key_near)
    for copy in att_copies + grad_copies:
        copy.wait_recv()
    att_own.wait()
    grad_own.wait()
    assert len(sent) <= COPIES
    for copy in sent:
        copy.wait_send()


def hand_over(att, dproj, dcache, att_out, dproj_out, dcache_out, sems):
    copies = [
        pltpu.make_async_copy(src, dst, sems.at[i])
        for i, (src, dst) in enumerate(((att, att_out), (dproj, dproj_out), (dcache, dcache_out)))
    ]
    for copy in copies:
        copy.start()
    for copy in copies:
        copy.wait()


def local(projected, grad_output, prompt_cache, segment_ids, segment_prompt):
    hbm = pl.BlockSpec(memory_space=pltpu.HBM)
    vmem = pl.BlockSpec(memory_space=pltpu.VMEM)
    smem = pl.BlockSpec(memory_space=pltpu.SMEM)
    block = (PROMPT_LEN, HEAD_DIM)
    results = (
        jax.ShapeDtypeStruct(grad_output.shape, BF16),
        jax.ShapeDtypeStruct(projected.shape, BF16),
        jax.ShapeDtypeStruct(prompt_cache.shape, BF16),
    )
    outs = pl.pallas_call(
        kernel,
        out_shape=tuple(pltpu.VMEM(r.shape, BF16) for r in results),
        in_specs=[vmem, smem, hbm, hbm, hbm],
        out_specs=(vmem, vmem, vmem),
        scratch_shapes=[
            pltpu.VMEM((N_HEAD, ROWS, PACK), BF16),
            pltpu.VMEM((N_HEAD, ROWS, OUT), BF16),
            pltpu.VMEM((9,) + block, BF16),
            pltpu.VMEM((9,) + block, BF16),
            pltpu.VMEM((SEGS, GROUP, SEG_MOST, HEAD_DIM), BF16),
            pltpu.VMEM((2, SEGS, HEAD_DIM, HEAD_DIM), BF16),
            pltpu.VMEM((SEGS, GROUP, SEG_MOST, HEAD_DIM), BF16),
            pltpu.VMEM((SEGS, STACK, KEYS), F32),
            pltpu.VMEM((SEGS, STACK, KEYS), BF16),
            pltpu.VMEM((SEGS, STACK, KEYS), BF16),
            pltpu.VMEM((2, SEGS) + block, F32),
            pltpu.VMEM((SEGS, GROUP, SEG_MOST, HEAD_DIM), BF16),
            pltpu.VMEM((SEGS, GROUP + 2, SEG_MOST, HEAD_DIM), BF16),
            pltpu.VMEM((N_HEAD, ROWS, OUT), BF16),
            pltpu.VMEM((N_HEAD, ROWS, PACK), BF16),
            pltpu.VMEM((2, 4) + block, BF16),
            pltpu.VMEM((2, 4) + block, BF16),
            pltpu.VMEM((2, 2) + block, BF16),
            pltpu.VMEM((2, 2) + block, BF16),
            pltpu.VMEM((2, 2) + block, BF16),
            pltpu.VMEM((2, 2) + block, BF16),
            pltpu.SemaphoreType.DMA((4,)),
            pltpu.SemaphoreType.DMA((COPIES,)),
            pltpu.SemaphoreType.DMA((COPIES,)),
        ],
        compiler_params=pltpu.CompilerParams(
            collective_id=0, has_side_effects=True, vmem_limit_bytes=60 << 20
        ),
    )(segment_ids, segment_prompt, projected, grad_output, prompt_cache)
    return pl.pallas_call(
        hand_over,
        out_shape=results,
        in_specs=[vmem] * 3,
        out_specs=(hbm,) * 3,
        scratch_shapes=[pltpu.SemaphoreType.DMA((3,))],
        compiler_params=pltpu.CompilerParams(vmem_limit_bytes=8 << 20),
    )(*outs)


def solution(mesh):
    return jax.shard_map(
        local,
        mesh=mesh,
        in_specs=(
            P(("dp", "head"), None),
            P(("dp", "head"), None),
            P("dp", "head"),
            P("dp", None),
            P("dp", None),
        ),
        out_specs=(P(("dp", "head"), None), P(("dp", "head"), None), P("dp", "head")),
        check_vma=False,
    )
```

```python
import jax
import jax.numpy as jnp
from jax import lax
from jax.experimental import pallas as pl
from jax.experimental.pallas import tpu as pltpu
from jax.sharding import PartitionSpec as P

HEADS = 40
KV_HEADS = 8
HEAD_DIM = 128
GROUP = HEADS // KV_HEADS
TOK_DEV = 128
PROMPT_LEN = 512
SEGS = 4
REACH = 4
SEG_MOST = 64
N_DP = 64
CHIPS = N_DP // 2
N_HEAD = 8
ROWS = TOK_DEV // N_HEAD
PACK = (GROUP + 2) * HEAD_DIM
OUT = GROUP * HEAD_DIM
STACK = GROUP * SEG_MOST
KEYS = PROMPT_LEN + HEAD_DIM
SCALE = HEAD_DIM**-0.5
LOG2E = 1.4426950408889634
MESH = pl.DeviceIdType.MESH
F32 = jnp.float32
BF16 = jnp.bfloat16
COPIES = 80
HALF = PROMPT_LEN // 2


def dot(left, right, contract):
    return lax.dot_general(left, right, (contract, ((), ())), preferred_element_type=F32)


def kernel(
    ids_hbm, owner_hbm, proj, gout, cache,
    att_out, dproj_out, dcache_out,
    ids_ref, owner_ref, pk, dk, keys, values, win_q, win_kv, win_d, prob, prob_b, dscore_b, term, win_o, win_g, att_send, dproj_send,
    sib_send, sib_recv, far_send, far_recv, near_send, near_recv,
    local_sem, send_sem, recv_sem,
):
    dp = lax.axis_index("dp")
    head = lax.axis_index("head")
    chip = dp // 2
    core = lax.rem(dp, 2)
    sibling = (dp + 1 - 2 * core, head)
    right = (lax.rem(chip + 1, CHIPS) * 2 + core, head)
    left = (lax.rem(chip + CHIPS - 1, CHIPS) * 2 + core, head)
    peers = [lax.rem(head + j, N_HEAD) for j in (4, 3, 5, 2, 6, 1, 7)]
    kv = (keys, values)
    sent = []

    def send(src, dst, device):
        i = len(sent)
        copy = pltpu.make_async_remote_copy(
            src_ref=src, dst_ref=dst, send_sem=send_sem.at[i], recv_sem=recv_sem.at[i],
            device_id=device, device_id_type=MESH,
        )
        copy.start()
        sent.append(copy)
        return copy

    def columns(index, width):
        return pl.ds(pl.multiple_of(index * width, HEAD_DIM), width)

    def feature(w):
        return pl.ds(w * HEAD_DIM, HEAD_DIM)

    halves = [pl.ds(i * HALF, HALF) for i in range(2)]

    barrier = pltpu.get_barrier_semaphore()
    partners = [right, left] + [(dp, p) for p in peers] + [sibling]
    for partner in partners:
        pl.semaphore_signal(barrier, inc=1, device_id=partner, device_id_type=MESH)
    small = [
        pltpu.make_async_copy(ids_hbm, ids_ref, local_sem.at[4]),
        pltpu.make_async_copy(owner_hbm, owner_ref, local_sem.at[5]),
    ]
    own_kv = [pltpu.make_async_copy(cache.at[:, feature(w)], kv[w].at[2], local_sem.at[w]) for w in range(2)]
    own_proj = pltpu.make_async_copy(proj.at[:, columns(head, PACK)], pk.at[head], local_sem.at[2])
    own_gout = pltpu.make_async_copy(gout.at[:, columns(head, OUT)], dk.at[head], local_sem.at[3])
    for copy in small + own_kv + [own_proj, own_gout]:
        copy.start()
    for copy in small:
        copy.wait()

    ids = ids_ref[...]
    position = lax.broadcasted_iota(jnp.int32, (1, TOK_DEV), 1)
    first = jnp.zeros((1, TOK_DEV), jnp.int32)
    for s in range(SEGS):
        before = jnp.sum((ids < s).astype(jnp.int32), axis=1, keepdims=True)
        first = first + jnp.where(ids == s, before, 0)
    row = (ids * SEG_MOST + position - first).astype(F32)
    rows = lax.broadcasted_iota(jnp.int32, (SEGS * SEG_MOST, TOK_DEV), 0).astype(F32)
    pick = (jnp.broadcast_to(row, rows.shape) == rows).astype(BF16)
    row_t = jnp.transpose(jnp.broadcast_to(row, (TOK_DEV, TOK_DEV)))
    cols = lax.broadcasted_iota(jnp.int32, (TOK_DEV, SEGS * SEG_MOST), 1).astype(F32)
    unpick = (jnp.concatenate([row_t, row_t], axis=1) == cols).astype(BF16)

    offsets, slots = [], []
    for s in range(SEGS):
        offset = lax.rem(owner_ref[0, s] - dp + N_DP + REACH, N_DP) - REACH
        odd = lax.rem(offset + 8, 2)
        away = jnp.where(odd == 1, offset - 1 + 2 * core, offset) // 2
        slot = jnp.where(
            odd == 0, jnp.clip(away, -2, 2) + 2,
            jnp.where(away == 0, 5, jnp.where(away == 1, 6, jnp.where(away == -1, 7, 8))),
        )
        offsets.append(offset)
        slots.append(slot)

    pl.semaphore_wait(barrier, len(partners))

    def start_near(w):
        copies = []
        for half in halves:
            block = cache.at[half, feature(w)]
            copies.append(send(block, kv[w].at[1, half], right))
            copies.append(send(block, kv[w].at[3, half], left))
        return copies

    def relay(w, i, near):
        near[2 * i].wait_recv()
        from_left = send(kv[w].at[1, halves[i]], kv[w].at[0, halves[i]], right)
        near[2 * i + 1].wait_recv()
        from_right = send(kv[w].at[3, halves[i]], kv[w].at[4, halves[i]], left)
        return [from_left, from_right]

    def share_near(w):
        return [send(kv[w].at[1], kv[w].at[7], sibling), send(kv[w].at[3], kv[w].at[6], sibling)]

    def share_far(w, far):
        for copy in far:
            copy.wait_recv()
        return [send(kv[w].at[4 - 4 * core], kv[w].at[8], sibling)]

    near_k = start_near(0)
    sib_k = [send(cache.at[:, feature(0)], keys.at[5], sibling)]
    a2a_p = [send(proj.at[:, columns(p, PACK)], pk.at[head], (dp, p)) for p in peers]
    far_k = relay(0, 0, near_k)
    far_k += relay(0, 1, near_k)
    near_v = start_near(1)
    sib_k += share_near(0)
    a2a_g = [send(gout.at[:, columns(p, OUT)], dk.at[head], (dp, p)) for p in peers]
    sib_v = [send(cache.at[:, feature(1)], values.at[5], sibling)]

    def spread(picked, window):
        for g in range(GROUP):
            part = picked[:, g * HEAD_DIM : (g + 1) * HEAD_DIM]
            window[:, g] = part.reshape(SEGS, SEG_MOST, HEAD_DIM)

    def gather_proj():
        own_proj.wait()
        for copy in a2a_p:
            copy.wait_recv()
        picked = dot(pick, pk[...].reshape(TOK_DEV, PACK), ((1,), (0,))).astype(BF16)
        spread(picked, win_q)
        for w in range(2):
            own = picked[:, OUT + w * HEAD_DIM : OUT + (w + 1) * HEAD_DIM].reshape(SEGS, SEG_MOST, HEAD_DIM)
            win_kv[w] = jnp.concatenate([own, jnp.zeros_like(own)], axis=1)

    def gather_gout():
        own_gout.wait()
        for copy in a2a_g:
            copy.wait_recv()
        spread(dot(pick, dk[...].reshape(TOK_DEV, OUT), ((1,), (0,))).astype(BF16), win_d)

    def all_rows(w, s):
        return jnp.concatenate([kv[w][slots[s]], win_kv[w, s]], axis=0)

    def queries(s):
        return win_q[s].reshape(STACK, HEAD_DIM)

    def dout(s):
        return win_d[s].reshape(STACK, HEAD_DIM)

    key_at = lax.broadcasted_iota(jnp.int32, (STACK, HEAD_DIM), 1)
    row_at = lax.rem(lax.broadcasted_iota(jnp.int32, (STACK, HEAD_DIM), 0), SEG_MOST)

    def weigh(s):
        scores = dot(queries(s), all_rows(0, s), ((1,), (1,)))
        own = jnp.where(key_at <= row_at, scores[:, PROMPT_LEN:], -1e30)
        scores = jnp.concatenate([scores[:, :PROMPT_LEN], own], axis=1)
        top = jnp.max(scores, axis=1, keepdims=True)
        expo = jnp.exp2((scores - top) * (SCALE * LOG2E))
        weights = expo * (1.0 / jnp.sum(expo, axis=1, keepdims=True))
        prob[s] = weights
        prob_b[s] = weights.astype(BF16)

    def value_terms(s):
        dvalue = dot(prob_b[s], dout(s), ((0,), (0,)))
        term[1, s] = dvalue[:PROMPT_LEN]
        win_g[s, GROUP + 1] = dvalue[PROMPT_LEN : PROMPT_LEN + SEG_MOST].astype(BF16)

    def attend(s):
        out = dot(prob_b[s], all_rows(1, s), ((1,), (0,))).astype(BF16)
        win_o[s] = out.reshape(GROUP, SEG_MOST, HEAD_DIM)

    def key_terms(s):
        out = win_o[s].reshape(STACK, HEAD_DIM)
        delta = jnp.sum(dout(s).astype(F32) * out.astype(F32), axis=1, keepdims=True)
        dweight = dot(dout(s), all_rows(1, s), ((1,), (1,)))
        dscore = (prob[s] * (dweight - delta) * SCALE).astype(BF16)
        dscore_b[s] = dscore
        dkey = dot(dscore, queries(s), ((0,), (0,)))
        term[0, s] = dkey[:PROMPT_LEN]
        win_g[s, GROUP] = dkey[PROMPT_LEN : PROMPT_LEN + SEG_MOST].astype(BF16)

    def query_terms(s):
        dquery = dot(dscore_b[s], all_rows(0, s), ((1,), (0,))).astype(BF16)
        win_g[s, :GROUP] = dquery.reshape(GROUP, SEG_MOST, HEAD_DIM)

    def summed(w, offset, part):
        total = jnp.zeros((part.size, HEAD_DIM), F32)
        for s in range(SEGS):
            total = total + jnp.where(offsets[s] == offset, term[w, s, part], 0.0)
        return total

    whole = pl.ds(0, PROMPT_LEN)

    def to_sibling(w):
        copies = [None] * 4
        for i, offset in ((3, 6 * core - 3), (0, -1 - 2 * core), (2, 3 - 2 * core), (1, 1 - 2 * core)):
            sib_send[w, i] = summed(w, offset, whole).astype(BF16)
            copies[i] = send(sib_send.at[w, i], sib_recv.at[w, i], sibling)
        return copies

    def to_far(w, sib):
        sib[3].wait_recv()
        copies = []
        for half in halves:
            extra = sib_recv[w, 3, half].astype(F32)
            far_send[w, 0, half] = (summed(w, 4, half) + jnp.where(core == 0, extra, 0.0)).astype(BF16)
            copies.append(send(far_send.at[w, 0, half], far_recv.at[w, 0, half], right))
            far_send[w, 1, half] = (summed(w, -4, half) + jnp.where(core == 1, extra, 0.0)).astype(BF16)
            copies.append(send(far_send.at[w, 1, half], far_recv.at[w, 1, half], left))
        return copies

    def to_near(w, h, sib, far):
        half = halves[h]
        copies = []
        for i, device in enumerate((right, left)):
            if h == 0:
                sib[2 - 2 * i].wait_recv()
            part = summed(w, 2 - 4 * i, half) + sib_recv[w, 2 - 2 * i, half].astype(F32)
            far[2 * h + i].wait_recv()
            near_send[w, i, half] = (part + far_recv[w, i, half].astype(F32)).astype(BF16)
            copies.append(send(near_send.at[w, i, half], near_recv.at[w, i, half], device))
        return copies

    def finish(w, h, sib, near):
        half = halves[h]
        if h == 0:
            sib[1].wait_recv()
        total = summed(w, 0, half) + sib_recv[w, 1, half].astype(F32)
        for i in range(2):
            near[2 * h + i].wait_recv()
            total = total + near_recv[w, i, half].astype(F32)
        dcache_out[half, feature(w)] = total.astype(BF16)

    def give_back(window, staged, out, width, sem):
        parts = [window[:, g].reshape(SEGS * SEG_MOST, HEAD_DIM) for g in range(width // HEAD_DIM)]
        tokens = dot(unpick, jnp.concatenate(parts, axis=1), ((1,), (0,)))
        staged[...] = tokens.astype(BF16).reshape(N_HEAD, ROWS, width)
        copies = [send(staged.at[p], out.at[:, columns(head, width)], (dp, p)) for p in peers]
        own = pltpu.make_async_copy(staged.at[head], out.at[:, columns(head, width)], local_sem.at[sem])
        own.start()
        return copies, own

    gather_proj()
    sib_k += share_far(0, far_k)
    own_kv[0].wait()
    for copy in sib_k:
        copy.wait_recv()
    far_v = relay(1, 0, near_v)
    weigh(0)
    weigh(1)
    far_v += relay(1, 1, near_v)
    sib_v += share_near(1)
    weigh(2)
    weigh(3)
    gather_gout()
    for s in range(SEGS):
        value_terms(s)
    value_sib = to_sibling(1)
    sib_v += share_far(1, far_v)
    value_far = to_far(1, value_sib)
    own_kv[1].wait()
    for copy in sib_v:
        copy.wait_recv()
    for s in range(SEGS):
        attend(s)
    att_copies, att_own = give_back(win_o, att_send, att_out, OUT, 0)
    for s in range(SEGS):
        key_terms(s)
    key_sib = to_sibling(0)
    for s in range(SEGS):
        query_terms(s)
    grad_copies, grad_own = give_back(win_g, dproj_send, dproj_out, PACK, 1)
    key_far = to_far(0, key_sib)
    value_near = to_near(1, 0, value_sib, value_far)
    value_near += to_near(1, 1, value_sib, value_far)
    key_near = to_near(0, 0, key_sib, key_far)
    key_near += to_near(0, 1, key_sib, key_far)
    finish(1, 0, value_sib, value_near)
    finish(1, 1, value_sib, value_near)
    finish(0, 0, key_sib, key_near)
    finish(0, 1, key_sib, key_near)
    for copy in att_copies + grad_copies:
        copy.wait_recv()
    att_own.wait()
    grad_own.wait()
    assert len(sent) <= COPIES
    for copy in sent:
        copy.wait_send()


def hand_over(att, dproj, dcache, att_out, dproj_out, dcache_out, sems):
    copies = [
        pltpu.make_async_copy(src, dst, sems.at[i])
        for i, (src, dst) in enumerate(((att, att_out), (dproj, dproj_out), (dcache, dcache_out)))
    ]
    for copy in copies:
        copy.start()
    for copy in copies:
        copy.wait()


def local(projected, grad_output, prompt_cache, segment_ids, segment_prompt):
    hbm = pl.BlockSpec(memory_space=pltpu.HBM)
    vmem = pl.BlockSpec(memory_space=pltpu.VMEM)
    block = (PROMPT_LEN, HEAD_DIM)
    results = (
        jax.ShapeDtypeStruct(grad_output.shape, BF16),
        jax.ShapeDtypeStruct(projected.shape, BF16),
        jax.ShapeDtypeStruct(prompt_cache.shape, BF16),
    )
    outs = pl.pallas_call(
        kernel,
        out_shape=tuple(pltpu.VMEM(r.shape, BF16) for r in results),
        in_specs=[hbm] * 5,
        out_specs=(vmem, vmem, vmem),
        scratch_shapes=[
            pltpu.VMEM(segment_ids.shape, jnp.int32),
            pltpu.SMEM(segment_prompt.shape, jnp.int32),
            pltpu.VMEM((N_HEAD, ROWS, PACK), BF16),
            pltpu.VMEM((N_HEAD, ROWS, OUT), BF16),
            pltpu.VMEM((9,) + block, BF16),
            pltpu.VMEM((9,) + block, BF16),
            pltpu.VMEM((SEGS, GROUP, SEG_MOST, HEAD_DIM), BF16),
            pltpu.VMEM((2, SEGS, HEAD_DIM, HEAD_DIM), BF16),
            pltpu.VMEM((SEGS, GROUP, SEG_MOST, HEAD_DIM), BF16),
            pltpu.VMEM((SEGS, STACK, KEYS), F32),
            pltpu.VMEM((SEGS, STACK, KEYS), BF16),
            pltpu.VMEM((SEGS, STACK, KEYS), BF16),
            pltpu.VMEM((2, SEGS) + block, F32),
            pltpu.VMEM((SEGS, GROUP, SEG_MOST, HEAD_DIM), BF16),
            pltpu.VMEM((SEGS, GROUP + 2, SEG_MOST, HEAD_DIM), BF16),
            pltpu.VMEM((N_HEAD, ROWS, OUT), BF16),
            pltpu.VMEM((N_HEAD, ROWS, PACK), BF16),
            pltpu.VMEM((2, 4) + block, BF16),
            pltpu.VMEM((2, 4) + block, BF16),
            pltpu.VMEM((2, 2) + block, BF16),
            pltpu.VMEM((2, 2) + block, BF16),
            pltpu.VMEM((2, 2) + block, BF16),
            pltpu.VMEM((2, 2) + block, BF16),
            pltpu.SemaphoreType.DMA((6,)),
            pltpu.SemaphoreType.DMA((COPIES,)),
            pltpu.SemaphoreType.DMA((COPIES,)),
        ],
        compiler_params=pltpu.CompilerParams(
            collective_id=0, has_side_effects=True, vmem_limit_bytes=60 << 20
        ),
    )(segment_ids, segment_prompt, projected, grad_output, prompt_cache)
    return pl.pallas_call(
        hand_over,
        out_shape=results,
        in_specs=[vmem] * 3,
        out_specs=(hbm,) * 3,
        scratch_shapes=[pltpu.SemaphoreType.DMA((3,))],
        compiler_params=pltpu.CompilerParams(vmem_limit_bytes=8 << 20),
    )(*outs)


def solution(mesh):
    return jax.shard_map(
        local,
        mesh=mesh,
        in_specs=(
            P(("dp", "head"), None),
            P(("dp", "head"), None),
            P("dp", "head"),
            P("dp", None),
            P("dp", None),
        ),
        out_specs=(P(("dp", "head"), None), P(("dp", "head"), None), P("dp", "head")),
        check_vma=False,
    )
```

```python
import jax
import jax.numpy as jnp
from jax import lax
from jax.experimental import pallas as pl
from jax.experimental.pallas import tpu as pltpu
from jax.sharding import PartitionSpec as P

HEADS = 40
KV_HEADS = 8
HEAD_DIM = 128
GROUP = HEADS // KV_HEADS
TOK_DEV = 128
PROMPT_LEN = 512
SEGS = 4
REACH = 4
SEG_MOST = 64
N_DP = 64
CHIPS = N_DP // 2
N_HEAD = 8
ROWS = TOK_DEV // N_HEAD
PACK = (GROUP + 2) * HEAD_DIM
OUT = GROUP * HEAD_DIM
STACK = GROUP * SEG_MOST
KEYS = PROMPT_LEN + HEAD_DIM
SCALE = HEAD_DIM**-0.5
LOG2E = 1.4426950408889634
MESH = pl.DeviceIdType.MESH
F32 = jnp.float32
BF16 = jnp.bfloat16
COPIES = 80
HALF = PROMPT_LEN // 2


def dot(left, right, contract):
    return lax.dot_general(left, right, (contract, ((), ())), preferred_element_type=F32)


def kernel(
    ids_hbm, owner_hbm, proj, gout, cache,
    att_out, dproj_out, dcache_out,
    ids_ref, owner_ref, pk, dk, keys, values, win_q, win_kv, win_d, prob, prob_b, dscore_b, term, win_o, win_g, att_send, dproj_send,
    sib_send, sib_recv, far_send, far_recv, near_send, near_recv,
    local_sem, send_sem, recv_sem, ring_sem,
):
    dp = lax.axis_index("dp")
    head = lax.axis_index("head")
    chip = dp // 2
    core = lax.rem(dp, 2)
    sibling = (dp + 1 - 2 * core, head)
    right = (lax.rem(chip + 1, CHIPS) * 2 + core, head)
    left = (lax.rem(chip + CHIPS - 1, CHIPS) * 2 + core, head)
    peers = [lax.rem(head + j, N_HEAD) for j in (1, 7, 2, 6, 3, 5, 4)]
    kv = (keys, values)
    sent = []

    def send(src, dst, device):
        i = len(sent)
        copy = pltpu.make_async_remote_copy(
            src_ref=src, dst_ref=dst, send_sem=send_sem.at[i], recv_sem=recv_sem.at[i],
            device_id=device, device_id_type=MESH,
        )
        copy.start()
        sent.append(copy)
        return copy

    def columns(index, width):
        return pl.ds(pl.multiple_of(index * width, HEAD_DIM), width)

    def feature(w):
        return pl.ds(w * HEAD_DIM, HEAD_DIM)

    halves = [pl.ds(i * HALF, HALF) for i in range(2)]

    barrier = pltpu.get_barrier_semaphore()
    partners = [right, left, (dp, peers[0]), (dp, peers[1]), sibling]
    for partner in partners:
        pl.semaphore_signal(barrier, inc=1, device_id=partner, device_id_type=MESH)
    small = [
        pltpu.make_async_copy(ids_hbm, ids_ref, local_sem.at[4]),
        pltpu.make_async_copy(owner_hbm, owner_ref, local_sem.at[5]),
    ]
    own_kv = [pltpu.make_async_copy(cache.at[:, feature(w)], kv[w].at[2], local_sem.at[w]) for w in range(2)]
    own_proj = pltpu.make_async_copy(proj.at[:, columns(head, PACK)], pk.at[head], local_sem.at[2])
    own_gout = pltpu.make_async_copy(gout.at[:, columns(head, OUT)], dk.at[head], local_sem.at[3])
    for copy in small + own_kv + [own_proj, own_gout]:
        copy.start()
    for copy in small:
        copy.wait()

    ids = ids_ref[...]
    position = lax.broadcasted_iota(jnp.int32, (1, TOK_DEV), 1)
    first = jnp.zeros((1, TOK_DEV), jnp.int32)
    for s in range(SEGS):
        before = jnp.sum((ids < s).astype(jnp.int32), axis=1, keepdims=True)
        first = first + jnp.where(ids == s, before, 0)
    row = (ids * SEG_MOST + position - first).astype(F32)
    rows = lax.broadcasted_iota(jnp.int32, (SEGS * SEG_MOST, TOK_DEV), 0).astype(F32)
    pick = (jnp.broadcast_to(row, rows.shape) == rows).astype(BF16)
    row_t = jnp.transpose(jnp.broadcast_to(row, (TOK_DEV, TOK_DEV)))
    cols = lax.broadcasted_iota(jnp.int32, (TOK_DEV, SEGS * SEG_MOST), 1).astype(F32)
    unpick = (jnp.concatenate([row_t, row_t], axis=1) == cols).astype(BF16)

    offsets, slots = [], []
    for s in range(SEGS):
        offset = lax.rem(owner_ref[0, s] - dp + N_DP + REACH, N_DP) - REACH
        odd = lax.rem(offset + 8, 2)
        away = jnp.where(odd == 1, offset - 1 + 2 * core, offset) // 2
        slot = jnp.where(
            odd == 0, jnp.clip(away, -2, 2) + 2,
            jnp.where(away == 0, 5, jnp.where(away == 1, 6, jnp.where(away == -1, 7, 8))),
        )
        offsets.append(offset)
        slots.append(slot)

    pl.semaphore_wait(barrier, len(partners))

    def start_near(w):
        copies = []
        for half in halves:
            block = cache.at[half, feature(w)]
            copies.append(send(block, kv[w].at[1, half], right))
            copies.append(send(block, kv[w].at[3, half], left))
        return copies

    def relay(w, i, near):
        near[2 * i].wait_recv()
        from_left = send(kv[w].at[1, halves[i]], kv[w].at[0, halves[i]], right)
        near[2 * i + 1].wait_recv()
        from_right = send(kv[w].at[3, halves[i]], kv[w].at[4, halves[i]], left)
        return [from_left, from_right]

    def share_near(w):
        return [send(kv[w].at[1], kv[w].at[7], sibling), send(kv[w].at[3], kv[w].at[6], sibling)]

    def share_far(w, far):
        for copy in far:
            copy.wait_recv()
        return [send(kv[w].at[4 - 4 * core], kv[w].at[8], sibling)]

    near_k = start_near(0)
    near_v = start_near(1)
    sib_k = [send(cache.at[:, feature(0)], keys.at[5], sibling)]
    sib_v = [send(cache.at[:, feature(1)], values.at[5], sibling)]

    def next_round():
        for i in range(2):
            pl.semaphore_signal(ring_sem.at[i], inc=1, device_id=(dp, peers[i]), device_id_type=MESH)
        for i in range(2):
            pl.semaphore_wait(ring_sem.at[i], 1)

    def exchange(block, staged, width, chosen):
        return [send(block.at[:, columns(p, width)], staged.at[head], (dp, p)) for p in chosen]

    a2a_p = exchange(proj, pk, PACK, peers[:2])
    a2a_g = []
    for distance in range(1, 4):
        next_round()
        a2a_p += exchange(proj, pk, PACK, peers[2 * distance : 2 * distance + 2])
    a2a_g += exchange(gout, dk, OUT, peers)
    far_k = relay(0, 0, near_k)
    far_k += relay(0, 1, near_k)
    sib_k += share_near(0)
    far_v = relay(1, 0, near_v)
    far_v += relay(1, 1, near_v)
    sib_v += share_near(1)

    def spread(picked, window):
        for g in range(GROUP):
            part = picked[:, g * HEAD_DIM : (g + 1) * HEAD_DIM]
            window[:, g] = part.reshape(SEGS, SEG_MOST, HEAD_DIM)

    def gather_proj():
        own_proj.wait()
        for copy in a2a_p:
            copy.wait_recv()
        picked = dot(pick, pk[...].reshape(TOK_DEV, PACK), ((1,), (0,))).astype(BF16)
        spread(picked, win_q)
        for w in range(2):
            own = picked[:, OUT + w * HEAD_DIM : OUT + (w + 1) * HEAD_DIM].reshape(SEGS, SEG_MOST, HEAD_DIM)
            win_kv[w] = jnp.concatenate([own, jnp.zeros_like(own)], axis=1)

    def gather_gout():
        own_gout.wait()
        for copy in a2a_g:
            copy.wait_recv()
        spread(dot(pick, dk[...].reshape(TOK_DEV, OUT), ((1,), (0,))).astype(BF16), win_d)

    def all_rows(w, s):
        return jnp.concatenate([kv[w][slots[s]], win_kv[w, s]], axis=0)

    def queries(s):
        return win_q[s].reshape(STACK, HEAD_DIM)

    def dout(s):
        return win_d[s].reshape(STACK, HEAD_DIM)

    key_at = lax.broadcasted_iota(jnp.int32, (STACK, HEAD_DIM), 1)
    row_at = lax.rem(lax.broadcasted_iota(jnp.int32, (STACK, HEAD_DIM), 0), SEG_MOST)

    def weigh(s):
        scores = dot(queries(s), all_rows(0, s), ((1,), (1,)))
        own = jnp.where(key_at <= row_at, scores[:, PROMPT_LEN:], -1e30)
        scores = jnp.concatenate([scores[:, :PROMPT_LEN], own], axis=1)
        top = jnp.max(scores, axis=1, keepdims=True)
        expo = jnp.exp2((scores - top) * (SCALE * LOG2E))
        weights = expo * (1.0 / jnp.sum(expo, axis=1, keepdims=True))
        prob[s] = weights
        prob_b[s] = weights.astype(BF16)

    def value_terms(s):
        dvalue = dot(prob_b[s], dout(s), ((0,), (0,)))
        term[1, s] = dvalue[:PROMPT_LEN]
        win_g[s, GROUP + 1] = dvalue[PROMPT_LEN : PROMPT_LEN + SEG_MOST].astype(BF16)

    def attend(s):
        out = dot(prob_b[s], all_rows(1, s), ((1,), (0,))).astype(BF16)
        win_o[s] = out.reshape(GROUP, SEG_MOST, HEAD_DIM)

    def key_terms(s):
        out = win_o[s].reshape(STACK, HEAD_DIM)
        delta = jnp.sum(dout(s).astype(F32) * out.astype(F32), axis=1, keepdims=True)
        dweight = dot(dout(s), all_rows(1, s), ((1,), (1,)))
        dscore = (prob[s] * (dweight - delta) * SCALE).astype(BF16)
        dscore_b[s] = dscore
        dkey = dot(dscore, queries(s), ((0,), (0,)))
        term[0, s] = dkey[:PROMPT_LEN]
        win_g[s, GROUP] = dkey[PROMPT_LEN : PROMPT_LEN + SEG_MOST].astype(BF16)

    def query_terms(s):
        dquery = dot(dscore_b[s], all_rows(0, s), ((1,), (0,))).astype(BF16)
        win_g[s, :GROUP] = dquery.reshape(GROUP, SEG_MOST, HEAD_DIM)

    def summed(w, offset, part):
        total = jnp.zeros((part.size, HEAD_DIM), F32)
        for s in range(SEGS):
            total = total + jnp.where(offsets[s] == offset, term[w, s, part], 0.0)
        return total

    whole = pl.ds(0, PROMPT_LEN)

    def to_sibling(w):
        copies = [None] * 4
        for i, offset in ((3, 6 * core - 3), (0, -1 - 2 * core), (2, 3 - 2 * core), (1, 1 - 2 * core)):
            sib_send[w, i] = summed(w, offset, whole).astype(BF16)
            copies[i] = send(sib_send.at[w, i], sib_recv.at[w, i], sibling)
        return copies

    def to_far(w, sib):
        sib[3].wait_recv()
        copies = []
        for half in halves:
            extra = sib_recv[w, 3, half].astype(F32)
            far_send[w, 0, half] = (summed(w, 4, half) + jnp.where(core == 0, extra, 0.0)).astype(BF16)
            copies.append(send(far_send.at[w, 0, half], far_recv.at[w, 0, half], right))
            far_send[w, 1, half] = (summed(w, -4, half) + jnp.where(core == 1, extra, 0.0)).astype(BF16)
            copies.append(send(far_send.at[w, 1, half], far_recv.at[w, 1, half], left))
        return copies

    def to_near(w, h, sib, far):
        half = halves[h]
        copies = []
        for i, device in enumerate((right, left)):
            if h == 0:
                sib[2 - 2 * i].wait_recv()
            part = summed(w, 2 - 4 * i, half) + sib_recv[w, 2 - 2 * i, half].astype(F32)
            far[2 * h + i].wait_recv()
            near_send[w, i, half] = (part + far_recv[w, i, half].astype(F32)).astype(BF16)
            copies.append(send(near_send.at[w, i, half], near_recv.at[w, i, half], device))
        return copies

    def finish(w, h, sib, near):
        half = halves[h]
        if h == 0:
            sib[1].wait_recv()
        total = summed(w, 0, half) + sib_recv[w, 1, half].astype(F32)
        for i in range(2):
            near[2 * h + i].wait_recv()
            total = total + near_recv[w, i, half].astype(F32)
        dcache_out[half, feature(w)] = total.astype(BF16)

    def give_back(window, staged, out, width, sem):
        parts = [window[:, g].reshape(SEGS * SEG_MOST, HEAD_DIM) for g in range(width // HEAD_DIM)]
        tokens = dot(unpick, jnp.concatenate(parts, axis=1), ((1,), (0,)))
        staged[...] = tokens.astype(BF16).reshape(N_HEAD, ROWS, width)
        copies = [send(staged.at[p], out.at[:, columns(head, width)], (dp, p)) for p in peers]
        own = pltpu.make_async_copy(staged.at[head], out.at[:, columns(head, width)], local_sem.at[sem])
        own.start()
        return copies, own

    gather_proj()
    sib_k += share_far(0, far_k)
    own_kv[0].wait()
    for copy in sib_k:
        copy.wait_recv()
    for s in range(SEGS):
        weigh(s)
    gather_gout()
    for s in range(SEGS):
        value_terms(s)
    value_sib = to_sibling(1)
    sib_v += share_far(1, far_v)
    value_far = to_far(1, value_sib)
    own_kv[1].wait()
    for copy in sib_v:
        copy.wait_recv()
    for s in range(SEGS):
        attend(s)
    att_copies, att_own = give_back(win_o, att_send, att_out, OUT, 0)
    for s in range(SEGS):
        key_terms(s)
    key_sib = to_sibling(0)
    for s in range(SEGS):
        query_terms(s)
    grad_copies, grad_own = give_back(win_g, dproj_send, dproj_out, PACK, 1)
    key_far = to_far(0, key_sib)
    value_near = to_near(1, 0, value_sib, value_far)
    value_near += to_near(1, 1, value_sib, value_far)
    key_near = to_near(0, 0, key_sib, key_far)
    key_near += to_near(0, 1, key_sib, key_far)
    finish(1, 0, value_sib, value_near)
    finish(1, 1, value_sib, value_near)
    finish(0, 0, key_sib, key_near)
    finish(0, 1, key_sib, key_near)
    for copy in att_copies + grad_copies:
        copy.wait_recv()
    att_own.wait()
    grad_own.wait()
    assert len(sent) <= COPIES
    for copy in sent:
        copy.wait_send()


def hand_over(att, dproj, dcache, att_out, dproj_out, dcache_out, sems):
    copies = [
        pltpu.make_async_copy(src, dst, sems.at[i])
        for i, (src, dst) in enumerate(((att, att_out), (dproj, dproj_out), (dcache, dcache_out)))
    ]
    for copy in copies:
        copy.start()
    for copy in copies:
        copy.wait()


def local(projected, grad_output, prompt_cache, segment_ids, segment_prompt):
    hbm = pl.BlockSpec(memory_space=pltpu.HBM)
    vmem = pl.BlockSpec(memory_space=pltpu.VMEM)
    block = (PROMPT_LEN, HEAD_DIM)
    results = (
        jax.ShapeDtypeStruct(grad_output.shape, BF16),
        jax.ShapeDtypeStruct(projected.shape, BF16),
        jax.ShapeDtypeStruct(prompt_cache.shape, BF16),
    )
    outs = pl.pallas_call(
        kernel,
        out_shape=tuple(pltpu.VMEM(r.shape, BF16) for r in results),
        in_specs=[hbm] * 5,
        out_specs=(vmem, vmem, vmem),
        scratch_shapes=[
            pltpu.VMEM(segment_ids.shape, jnp.int32),
            pltpu.SMEM(segment_prompt.shape, jnp.int32),
            pltpu.VMEM((N_HEAD, ROWS, PACK), BF16),
            pltpu.VMEM((N_HEAD, ROWS, OUT), BF16),
            pltpu.VMEM((9,) + block, BF16),
            pltpu.VMEM((9,) + block, BF16),
            pltpu.VMEM((SEGS, GROUP, SEG_MOST, HEAD_DIM), BF16),
            pltpu.VMEM((2, SEGS, HEAD_DIM, HEAD_DIM), BF16),
            pltpu.VMEM((SEGS, GROUP, SEG_MOST, HEAD_DIM), BF16),
            pltpu.VMEM((SEGS, STACK, KEYS), F32),
            pltpu.VMEM((SEGS, STACK, KEYS), BF16),
            pltpu.VMEM((SEGS, STACK, KEYS), BF16),
            pltpu.VMEM((2, SEGS) + block, F32),
            pltpu.VMEM((SEGS, GROUP, SEG_MOST, HEAD_DIM), BF16),
            pltpu.VMEM((SEGS, GROUP + 2, SEG_MOST, HEAD_DIM), BF16),
            pltpu.VMEM((N_HEAD, ROWS, OUT), BF16),
            pltpu.VMEM((N_HEAD, ROWS, PACK), BF16),
            pltpu.VMEM((2, 4) + block, BF16),
            pltpu.VMEM((2, 4) + block, BF16),
            pltpu.VMEM((2, 2) + block, BF16),
            pltpu.VMEM((2, 2) + block, BF16),
            pltpu.VMEM((2, 2) + block, BF16),
            pltpu.VMEM((2, 2) + block, BF16),
            pltpu.SemaphoreType.DMA((6,)),
            pltpu.SemaphoreType.DMA((COPIES,)),
            pltpu.SemaphoreType.DMA((COPIES,)),
            pltpu.SemaphoreType.REGULAR((2,)),
        ],
        compiler_params=pltpu.CompilerParams(
            collective_id=0, has_side_effects=True, vmem_limit_bytes=60 << 20
        ),
    )(segment_ids, segment_prompt, projected, grad_output, prompt_cache)
    return pl.pallas_call(
        hand_over,
        out_shape=results,
        in_specs=[vmem] * 3,
        out_specs=(hbm,) * 3,
        scratch_shapes=[pltpu.SemaphoreType.DMA((3,))],
        compiler_params=pltpu.CompilerParams(vmem_limit_bytes=8 << 20),
    )(*outs)


def solution(mesh):
    return jax.shard_map(
        local,
        mesh=mesh,
        in_specs=(
            P(("dp", "head"), None),
            P(("dp", "head"), None),
            P("dp", "head"),
            P("dp", None),
            P("dp", None),
        ),
        out_specs=(P(("dp", "head"), None), P(("dp", "head"), None), P("dp", "head")),
        check_vma=False,
    )
```

```python
import jax
import jax.numpy as jnp
from jax import lax
from jax.experimental import pallas as pl
from jax.experimental.pallas import tpu as pltpu
from jax.sharding import PartitionSpec as P

HEADS = 40
KV_HEADS = 8
HEAD_DIM = 128
GROUP = HEADS // KV_HEADS
TOK_DEV = 128
PROMPT_LEN = 512
SEGS = 4
REACH = 4
SEG_MOST = 64
N_DP = 64
CHIPS = N_DP // 2
CHIPS_Z = 8
N_HEAD = 8
ROWS = TOK_DEV // N_HEAD
PACK = (GROUP + 2) * HEAD_DIM
OUT = GROUP * HEAD_DIM
STACK = GROUP * SEG_MOST
KEYS = PROMPT_LEN + HEAD_DIM
SCALE = HEAD_DIM**-0.5
LOG2E = 1.4426950408889634
MESH = pl.DeviceIdType.MESH
F32 = jnp.float32
BF16 = jnp.bfloat16
COPIES = 80
HALF = PROMPT_LEN // 2


def dot(left, right, contract):
    return lax.dot_general(left, right, (contract, ((), ())), preferred_element_type=F32)


def kernel(
    ids_hbm, owner_hbm, proj, gout, cache,
    att_out, dproj_out, dcache_out,
    ids_ref, owner_ref, pk, dk, keys, values, win_q, win_kv, win_d, prob, prob_b, dscore_b, term, win_o, win_g, att_send, dproj_send,
    sib_send, sib_recv, far_send, far_recv, near_send, near_recv,
    local_sem, send_sem, recv_sem, ring_sem,
):
    dp = lax.axis_index("dp")
    head = lax.axis_index("head")
    chip = dp // 2
    core = lax.rem(dp, 2)
    sibling = (dp + 1 - 2 * core, head)
    right = (lax.rem(chip + 1, CHIPS) * 2 + core, head)
    left = (lax.rem(chip + CHIPS - 1, CHIPS) * 2 + core, head)
    peers = [lax.rem(head + j, N_HEAD) for j in (1, 7, 2, 6, 3, 5, 4)]
    kv = (keys, values)
    sent = []

    def prepare(src, dst, device):
        i = len(sent)
        copy = pltpu.make_async_remote_copy(
            src_ref=src, dst_ref=dst, send_sem=send_sem.at[i], recv_sem=recv_sem.at[i],
            device_id=device, device_id_type=MESH,
        )
        sent.append(copy)
        return copy

    def send(src, dst, device):
        copy = prepare(src, dst, device)
        copy.start()
        return copy

    def columns(index, width):
        return pl.ds(pl.multiple_of(index * width, HEAD_DIM), width)

    def feature(w):
        return pl.ds(w * HEAD_DIM, HEAD_DIM)

    z = lax.rem(chip, CHIPS_Z)
    slow = (z == 0, z == CHIPS_Z - 1)
    fast = (z != 0, z != CHIPS_Z - 1)

    halves = [pl.ds(i * HALF, HALF) for i in range(2)]

    barrier = pltpu.get_barrier_semaphore()
    partners = [right, left, (dp, peers[0]), (dp, peers[1]), sibling]
    for partner in partners:
        pl.semaphore_signal(barrier, inc=1, device_id=partner, device_id_type=MESH)
    small = [
        pltpu.make_async_copy(ids_hbm, ids_ref, local_sem.at[4]),
        pltpu.make_async_copy(owner_hbm, owner_ref, local_sem.at[5]),
    ]
    own_kv = [pltpu.make_async_copy(cache.at[:, feature(w)], kv[w].at[2], local_sem.at[w]) for w in range(2)]
    own_proj = pltpu.make_async_copy(proj.at[:, columns(head, PACK)], pk.at[head], local_sem.at[2])
    own_gout = pltpu.make_async_copy(gout.at[:, columns(head, OUT)], dk.at[head], local_sem.at[3])
    for copy in small + own_kv + [own_proj, own_gout]:
        copy.start()
    for copy in small:
        copy.wait()

    ids = ids_ref[...]
    position = lax.broadcasted_iota(jnp.int32, (1, TOK_DEV), 1)
    first = jnp.zeros((1, TOK_DEV), jnp.int32)
    for s in range(SEGS):
        before = jnp.sum((ids < s).astype(jnp.int32), axis=1, keepdims=True)
        first = first + jnp.where(ids == s, before, 0)
    row = (ids * SEG_MOST + position - first).astype(F32)
    rows = lax.broadcasted_iota(jnp.int32, (SEGS * SEG_MOST, TOK_DEV), 0).astype(F32)
    pick = (jnp.broadcast_to(row, rows.shape) == rows).astype(BF16)
    row_t = jnp.transpose(jnp.broadcast_to(row, (TOK_DEV, TOK_DEV)))
    cols = lax.broadcasted_iota(jnp.int32, (TOK_DEV, SEGS * SEG_MOST), 1).astype(F32)
    unpick = (jnp.concatenate([row_t, row_t], axis=1) == cols).astype(BF16)

    offsets, slots = [], []
    for s in range(SEGS):
        offset = lax.rem(owner_ref[0, s] - dp + N_DP + REACH, N_DP) - REACH
        odd = lax.rem(offset + 8, 2)
        away = jnp.where(odd == 1, offset - 1 + 2 * core, offset) // 2
        slot = jnp.where(
            odd == 0, jnp.clip(away, -2, 2) + 2,
            jnp.where(away == 0, 5, jnp.where(away == 1, 6, jnp.where(away == -1, 7, 8))),
        )
        offsets.append(offset)
        slots.append(slot)

    pl.semaphore_wait(barrier, len(partners))

    def start_near(w):
        copies = []
        for half in halves:
            block = cache.at[half, feature(w)]
            copies.append(send(block, kv[w].at[1, half], right))
            copies.append(send(block, kv[w].at[3, half], left))
        return copies

    def plan_relay(w):
        copies = []
        for half in halves:
            copies.append(prepare(kv[w].at[1, half], kv[w].at[0, half], right))
            copies.append(prepare(kv[w].at[3, half], kv[w].at[4, half], left))
        return copies

    def relay(h, near, far, when):
        for side in range(2):

            @pl.when(when[side])
            def _():
                near[2 * h + side].wait_recv()
                far[2 * h + side].start()

    def share_near(w):
        return [send(kv[w].at[1], kv[w].at[7], sibling), send(kv[w].at[3], kv[w].at[6], sibling)]

    def share_far(w, far):
        for copy in far:
            copy.wait_recv()
        return [send(kv[w].at[4 - 4 * core], kv[w].at[8], sibling)]

    near_k = start_near(0)
    near_v = start_near(1)
    sib_k = [send(cache.at[:, feature(0)], keys.at[5], sibling)]
    sib_v = [send(cache.at[:, feature(1)], values.at[5], sibling)]

    def next_round():
        for i in range(2):
            pl.semaphore_signal(ring_sem.at[i], inc=1, device_id=(dp, peers[i]), device_id_type=MESH)
        for i in range(2):
            pl.semaphore_wait(ring_sem.at[i], 1)

    def exchange(block, staged, width, chosen):
        return [send(block.at[:, columns(p, width)], staged.at[head], (dp, p)) for p in chosen]

    a2a_p = exchange(proj, pk, PACK, peers[:2])
    a2a_g = []
    for distance in range(1, 4):
        next_round()
        a2a_p += exchange(proj, pk, PACK, peers[2 * distance : 2 * distance + 2])
    a2a_g += exchange(gout, dk, OUT, peers)
    far_k, far_v = plan_relay(0), plan_relay(1)
    for near, far in ((near_k, far_k), (near_v, far_v)):
        for h in range(2):
            relay(h, near, far, fast)
    for h in range(2):
        relay(h, near_k, far_k, slow)
    sib_k += share_near(0)
    for h in range(2):
        relay(h, near_v, far_v, slow)
    sib_v += share_near(1)

    def spread(picked, window):
        for g in range(GROUP):
            part = picked[:, g * HEAD_DIM : (g + 1) * HEAD_DIM]
            window[:, g] = part.reshape(SEGS, SEG_MOST, HEAD_DIM)

    def gather_proj():
        own_proj.wait()
        for copy in a2a_p:
            copy.wait_recv()
        picked = dot(pick, pk[...].reshape(TOK_DEV, PACK), ((1,), (0,))).astype(BF16)
        spread(picked, win_q)
        for w in range(2):
            own = picked[:, OUT + w * HEAD_DIM : OUT + (w + 1) * HEAD_DIM].reshape(SEGS, SEG_MOST, HEAD_DIM)
            win_kv[w] = jnp.concatenate([own, jnp.zeros_like(own)], axis=1)

    def gather_gout():
        own_gout.wait()
        for copy in a2a_g:
            copy.wait_recv()
        spread(dot(pick, dk[...].reshape(TOK_DEV, OUT), ((1,), (0,))).astype(BF16), win_d)

    def all_rows(w, s):
        return jnp.concatenate([kv[w][slots[s]], win_kv[w, s]], axis=0)

    def queries(s):
        return win_q[s].reshape(STACK, HEAD_DIM)

    def dout(s):
        return win_d[s].reshape(STACK, HEAD_DIM)

    key_at = lax.broadcasted_iota(jnp.int32, (STACK, HEAD_DIM), 1)
    row_at = lax.rem(lax.broadcasted_iota(jnp.int32, (STACK, HEAD_DIM), 0), SEG_MOST)

    def weigh(s):
        scores = dot(queries(s), all_rows(0, s), ((1,), (1,)))
        own = jnp.where(key_at <= row_at, scores[:, PROMPT_LEN:], -1e30)
        scores = jnp.concatenate([scores[:, :PROMPT_LEN], own], axis=1)
        top = jnp.max(scores, axis=1, keepdims=True)
        expo = jnp.exp2((scores - top) * (SCALE * LOG2E))
        weights = expo * (1.0 / jnp.sum(expo, axis=1, keepdims=True))
        prob[s] = weights
        prob_b[s] = weights.astype(BF16)

    def value_terms(s):
        dvalue = dot(prob_b[s], dout(s), ((0,), (0,)))
        term[1, s] = dvalue[:PROMPT_LEN]
        win_g[s, GROUP + 1] = dvalue[PROMPT_LEN : PROMPT_LEN + SEG_MOST].astype(BF16)

    def attend(s):
        out = dot(prob_b[s], all_rows(1, s), ((1,), (0,))).astype(BF16)
        win_o[s] = out.reshape(GROUP, SEG_MOST, HEAD_DIM)

    def key_terms(s):
        out = win_o[s].reshape(STACK, HEAD_DIM)
        delta = jnp.sum(dout(s).astype(F32) * out.astype(F32), axis=1, keepdims=True)
        dweight = dot(dout(s), all_rows(1, s), ((1,), (1,)))
        dscore = (prob[s] * (dweight - delta) * SCALE).astype(BF16)
        dscore_b[s] = dscore
        dkey = dot(dscore, queries(s), ((0,), (0,)))
        term[0, s] = dkey[:PROMPT_LEN]
        win_g[s, GROUP] = dkey[PROMPT_LEN : PROMPT_LEN + SEG_MOST].astype(BF16)

    def query_terms(s):
        dquery = dot(dscore_b[s], all_rows(0, s), ((1,), (0,))).astype(BF16)
        win_g[s, :GROUP] = dquery.reshape(GROUP, SEG_MOST, HEAD_DIM)

    def summed(w, offset, part):
        total = jnp.zeros((part.size, HEAD_DIM), F32)
        for s in range(SEGS):
            total = total + jnp.where(offsets[s] == offset, term[w, s, part], 0.0)
        return total

    whole = pl.ds(0, PROMPT_LEN)

    def to_sibling(w):
        copies = [None] * 4
        for i, offset in ((3, 6 * core - 3), (0, -1 - 2 * core), (2, 3 - 2 * core), (1, 1 - 2 * core)):
            sib_send[w, i] = summed(w, offset, whole).astype(BF16)
            copies[i] = send(sib_send.at[w, i], sib_recv.at[w, i], sibling)
        return copies

    def to_far(w, sib):
        sib[3].wait_recv()
        copies = []
        for half in halves:
            extra = sib_recv[w, 3, half].astype(F32)
            far_send[w, 0, half] = (summed(w, 4, half) + jnp.where(core == 0, extra, 0.0)).astype(BF16)
            copies.append(send(far_send.at[w, 0, half], far_recv.at[w, 0, half], right))
            far_send[w, 1, half] = (summed(w, -4, half) + jnp.where(core == 1, extra, 0.0)).astype(BF16)
            copies.append(send(far_send.at[w, 1, half], far_recv.at[w, 1, half], left))
        return copies

    def plan_near(w):
        copies = []
        for half in halves:
            copies += [prepare(near_send.at[w, i, half], near_recv.at[w, i, half], (right, left)[i]) for i in range(2)]
        return copies

    def to_near(w, h, sib, far, near, when):
        half = halves[h]
        for i in range(2):

            @pl.when(when[i])
            def _():
                part = summed(w, 2 - 4 * i, half) + sib_recv[w, 2 - 2 * i, half].astype(F32)
                far[2 * h + i].wait_recv()
                near_send[w, i, half] = (part + far_recv[w, i, half].astype(F32)).astype(BF16)
                near[2 * h + i].start()

    def finish(w, h, sib, near):
        half = halves[h]
        if h == 0:
            sib[1].wait_recv()
        total = summed(w, 0, half) + sib_recv[w, 1, half].astype(F32)
        for i in range(2):
            near[2 * h + i].wait_recv()
            total = total + near_recv[w, i, half].astype(F32)
        dcache_out[half, feature(w)] = total.astype(BF16)

    def give_back(window, staged, out, width, sem):
        parts = [window[:, g].reshape(SEGS * SEG_MOST, HEAD_DIM) for g in range(width // HEAD_DIM)]
        tokens = dot(unpick, jnp.concatenate(parts, axis=1), ((1,), (0,)))
        staged[...] = tokens.astype(BF16).reshape(N_HEAD, ROWS, width)
        copies = [send(staged.at[p], out.at[:, columns(head, width)], (dp, p)) for p in peers]
        own = pltpu.make_async_copy(staged.at[head], out.at[:, columns(head, width)], local_sem.at[sem])
        own.start()
        return copies, own

    sib_k += share_far(0, far_k)
    gather_proj()
    own_kv[0].wait()
    for copy in sib_k:
        copy.wait_recv()
    for s in range(SEGS):
        weigh(s)
    gather_gout()
    for s in range(SEGS):
        value_terms(s)
    value_sib = to_sibling(1)
    sib_v += share_far(1, far_v)
    value_far = to_far(1, value_sib)
    own_kv[1].wait()
    for copy in sib_v:
        copy.wait_recv()
    for s in range(SEGS):
        attend(s)
    att_copies, att_own = give_back(win_o, att_send, att_out, OUT, 0)
    for s in range(SEGS):
        key_terms(s)
    key_sib = to_sibling(0)
    value_near, key_near = plan_near(1), plan_near(0)
    value_sib[0].wait_recv()
    value_sib[2].wait_recv()
    to_near(1, 0, value_sib, value_far, value_near, fast)
    for s in range(SEGS):
        query_terms(s)
    grad_copies, grad_own = give_back(win_g, dproj_send, dproj_out, PACK, 1)
    key_far = to_far(0, key_sib)
    to_near(1, 1, value_sib, value_far, value_near, fast)
    for h in range(2):
        to_near(1, h, value_sib, value_far, value_near, slow)
    key_sib[0].wait_recv()
    key_sib[2].wait_recv()
    for when in (fast, slow):
        for h in range(2):
            to_near(0, h, key_sib, key_far, key_near, when)
    finish(1, 0, value_sib, value_near)
    finish(1, 1, value_sib, value_near)
    finish(0, 0, key_sib, key_near)
    finish(0, 1, key_sib, key_near)
    for copy in att_copies + grad_copies:
        copy.wait_recv()
    att_own.wait()
    grad_own.wait()
    assert len(sent) <= COPIES
    for copy in sent:
        copy.wait_send()


def hand_over(att, dproj, dcache, att_out, dproj_out, dcache_out, sems):
    copies = [
        pltpu.make_async_copy(src, dst, sems.at[i])
        for i, (src, dst) in enumerate(((att, att_out), (dproj, dproj_out), (dcache, dcache_out)))
    ]
    for copy in copies:
        copy.start()
    for copy in copies:
        copy.wait()


def local(projected, grad_output, prompt_cache, segment_ids, segment_prompt):
    hbm = pl.BlockSpec(memory_space=pltpu.HBM)
    vmem = pl.BlockSpec(memory_space=pltpu.VMEM)
    block = (PROMPT_LEN, HEAD_DIM)
    results = (
        jax.ShapeDtypeStruct(grad_output.shape, BF16),
        jax.ShapeDtypeStruct(projected.shape, BF16),
        jax.ShapeDtypeStruct(prompt_cache.shape, BF16),
    )
    outs = pl.pallas_call(
        kernel,
        out_shape=tuple(pltpu.VMEM(r.shape, BF16) for r in results),
        in_specs=[hbm] * 5,
        out_specs=(vmem, vmem, vmem),
        scratch_shapes=[
            pltpu.VMEM(segment_ids.shape, jnp.int32),
            pltpu.SMEM(segment_prompt.shape, jnp.int32),
            pltpu.VMEM((N_HEAD, ROWS, PACK), BF16),
            pltpu.VMEM((N_HEAD, ROWS, OUT), BF16),
            pltpu.VMEM((9,) + block, BF16),
            pltpu.VMEM((9,) + block, BF16),
            pltpu.VMEM((SEGS, GROUP, SEG_MOST, HEAD_DIM), BF16),
            pltpu.VMEM((2, SEGS, HEAD_DIM, HEAD_DIM), BF16),
            pltpu.VMEM((SEGS, GROUP, SEG_MOST, HEAD_DIM), BF16),
            pltpu.VMEM((SEGS, STACK, KEYS), F32),
            pltpu.VMEM((SEGS, STACK, KEYS), BF16),
            pltpu.VMEM((SEGS, STACK, KEYS), BF16),
            pltpu.VMEM((2, SEGS) + block, F32),
            pltpu.VMEM((SEGS, GROUP, SEG_MOST, HEAD_DIM), BF16),
            pltpu.VMEM((SEGS, GROUP + 2, SEG_MOST, HEAD_DIM), BF16),
            pltpu.VMEM((N_HEAD, ROWS, OUT), BF16),
            pltpu.VMEM((N_HEAD, ROWS, PACK), BF16),
            pltpu.VMEM((2, 4) + block, BF16),
            pltpu.VMEM((2, 4) + block, BF16),
            pltpu.VMEM((2, 2) + block, BF16),
            pltpu.VMEM((2, 2) + block, BF16),
            pltpu.VMEM((2, 2) + block, BF16),
            pltpu.VMEM((2, 2) + block, BF16),
            pltpu.SemaphoreType.DMA((6,)),
            pltpu.SemaphoreType.DMA((COPIES,)),
            pltpu.SemaphoreType.DMA((COPIES,)),
            pltpu.SemaphoreType.REGULAR((2,)),
        ],
        compiler_params=pltpu.CompilerParams(
            collective_id=0, has_side_effects=True, vmem_limit_bytes=60 << 20
        ),
    )(segment_ids, segment_prompt, projected, grad_output, prompt_cache)
    return pl.pallas_call(
        hand_over,
        out_shape=results,
        in_specs=[vmem] * 3,
        out_specs=(hbm,) * 3,
        scratch_shapes=[pltpu.SemaphoreType.DMA((3,))],
        compiler_params=pltpu.CompilerParams(vmem_limit_bytes=8 << 20),
    )(*outs)


def solution(mesh):
    return jax.shard_map(
        local,
        mesh=mesh,
        in_specs=(
            P(("dp", "head"), None),
            P(("dp", "head"), None),
            P("dp", "head"),
            P("dp", None),
            P("dp", None),
        ),
        out_specs=(P(("dp", "head"), None), P(("dp", "head"), None), P("dp", "head")),
        check_vma=False,
    )
```

```python
import jax
import jax.numpy as jnp
from jax import lax
from jax.experimental import pallas as pl
from jax.experimental.pallas import tpu as pltpu
from jax.sharding import PartitionSpec as P

HEADS = 40
KV_HEADS = 8
HEAD_DIM = 128
GROUP = HEADS // KV_HEADS
TOK_DEV = 128
PROMPT_LEN = 512
SEGS = 4
REACH = 4
SEG_MOST = 64
N_DP = 64
CHIPS = N_DP // 2
CHIPS_Z = 8
N_HEAD = 8
ROWS = TOK_DEV // N_HEAD
PACK = (GROUP + 2) * HEAD_DIM
OUT = GROUP * HEAD_DIM
STACK = GROUP * SEG_MOST
KEYS = PROMPT_LEN + HEAD_DIM
SCALE = HEAD_DIM**-0.5
LOG2E = 1.4426950408889634
MESH = pl.DeviceIdType.MESH
F32 = jnp.float32
BF16 = jnp.bfloat16
COPIES = 80
HALF = PROMPT_LEN // 2


def dot(left, right, contract):
    return lax.dot_general(left, right, (contract, ((), ())), preferred_element_type=F32)


def kernel(
    ids_hbm, owner_hbm, proj, gout, cache,
    att_out, dproj_out, dcache_out,
    ids_ref, owner_ref, pk, dk, keys, values, win_q, win_kv, win_d, prob, prob_b, dscore_b, term, win_o, win_g, att_send, dproj_send,
    sib_send, sib_recv, far_send, far_recv, near_send, near_recv,
    local_sem, send_sem, recv_sem, ring_sem,
):
    dp = lax.axis_index("dp")
    head = lax.axis_index("head")
    chip = dp // 2
    core = lax.rem(dp, 2)
    sibling = (dp + 1 - 2 * core, head)
    right = (lax.rem(chip + 1, CHIPS) * 2 + core, head)
    left = (lax.rem(chip + CHIPS - 1, CHIPS) * 2 + core, head)
    peers = [lax.rem(head + j, N_HEAD) for j in (1, 7, 2, 6, 3, 5, 4)]
    kv = (keys, values)
    sent = []

    def prepare(src, dst, device):
        i = len(sent)
        copy = pltpu.make_async_remote_copy(
            src_ref=src, dst_ref=dst, send_sem=send_sem.at[i], recv_sem=recv_sem.at[i],
            device_id=device, device_id_type=MESH,
        )
        sent.append(copy)
        return copy

    def send(src, dst, device):
        copy = prepare(src, dst, device)
        copy.start()
        return copy

    def columns(index, width):
        return pl.ds(pl.multiple_of(index * width, HEAD_DIM), width)

    def feature(w):
        return pl.ds(w * HEAD_DIM, HEAD_DIM)

    z = lax.rem(chip, CHIPS_Z)
    slow = (z == 0, z == CHIPS_Z - 1)
    fast = (z != 0, z != CHIPS_Z - 1)

    halves = [pl.ds(i * HALF, HALF) for i in range(2)]

    barrier = pltpu.get_barrier_semaphore()
    partners = [right, left, (dp, peers[0]), (dp, peers[1]), sibling]
    for partner in partners:
        pl.semaphore_signal(barrier, inc=1, device_id=partner, device_id_type=MESH)
    small = [
        pltpu.make_async_copy(ids_hbm, ids_ref, local_sem.at[4]),
        pltpu.make_async_copy(owner_hbm, owner_ref, local_sem.at[5]),
    ]
    own_kv = [pltpu.make_async_copy(cache.at[:, feature(w)], kv[w].at[2], local_sem.at[w]) for w in range(2)]
    own_proj = pltpu.make_async_copy(proj.at[:, columns(head, PACK)], pk.at[head], local_sem.at[2])
    own_gout = pltpu.make_async_copy(gout.at[:, columns(head, OUT)], dk.at[head], local_sem.at[3])
    for copy in small + own_kv + [own_proj, own_gout]:
        copy.start()
    for copy in small:
        copy.wait()

    ids = ids_ref[...]
    position = lax.broadcasted_iota(jnp.int32, (1, TOK_DEV), 1)
    first = jnp.zeros((1, TOK_DEV), jnp.int32)
    for s in range(SEGS):
        before = jnp.sum((ids < s).astype(jnp.int32), axis=1, keepdims=True)
        first = first + jnp.where(ids == s, before, 0)
    row = (ids * SEG_MOST + position - first).astype(F32)
    rows = lax.broadcasted_iota(jnp.int32, (SEGS * SEG_MOST, TOK_DEV), 0).astype(F32)
    pick = (jnp.broadcast_to(row, rows.shape) == rows).astype(BF16)
    row_t = jnp.transpose(jnp.broadcast_to(row, (TOK_DEV, TOK_DEV)))
    cols = lax.broadcasted_iota(jnp.int32, (TOK_DEV, SEGS * SEG_MOST), 1).astype(F32)
    unpick = (jnp.concatenate([row_t, row_t], axis=1) == cols).astype(BF16)

    offsets, slots = [], []
    for s in range(SEGS):
        offset = lax.rem(owner_ref[0, s] - dp + N_DP + REACH, N_DP) - REACH
        odd = lax.rem(offset + 8, 2)
        away = jnp.where(odd == 1, offset - 1 + 2 * core, offset) // 2
        slot = jnp.where(
            odd == 0, jnp.clip(away, -2, 2) + 2,
            jnp.where(away == 0, 5, jnp.where(away == 1, 6, jnp.where(away == -1, 7, 8))),
        )
        offsets.append(offset)
        slots.append(slot)

    pl.semaphore_wait(barrier, len(partners))

    def start_near(w):
        copies = []
        for half in halves:
            block = cache.at[half, feature(w)]
            copies.append(send(block, kv[w].at[1, half], right))
            copies.append(send(block, kv[w].at[3, half], left))
        return copies

    def plan_relay(w):
        copies = []
        for half in halves:
            copies.append(prepare(kv[w].at[1, half], kv[w].at[0, half], right))
            copies.append(prepare(kv[w].at[3, half], kv[w].at[4, half], left))
        return copies

    def relay(h, near, far, when):
        for side in range(2):

            @pl.when(when[side])
            def _():
                near[2 * h + side].wait_recv()
                far[2 * h + side].start()

    def share_near(w):
        return [send(kv[w].at[1], kv[w].at[7], sibling), send(kv[w].at[3], kv[w].at[6], sibling)]

    def share_far(w, far):
        for copy in far:
            copy.wait_recv()
        return [send(kv[w].at[4 - 4 * core], kv[w].at[8], sibling)]

    near_k = start_near(0)
    near_v = start_near(1)
    sib_k = [send(cache.at[:, feature(0)], keys.at[5], sibling)]
    sib_v = [send(cache.at[:, feature(1)], values.at[5], sibling)]

    def next_round():
        for i in range(2):
            pl.semaphore_signal(ring_sem.at[i], inc=1, device_id=(dp, peers[i]), device_id_type=MESH)
        for i in range(2):
            pl.semaphore_wait(ring_sem.at[i], 1)

    def exchange(block, staged, width, chosen):
        return [send(block.at[:, columns(p, width)], staged.at[head], (dp, p)) for p in chosen]

    a2a_p = exchange(proj, pk, PACK, peers[:2])
    a2a_g = exchange(gout, dk, OUT, peers[:2])
    for distance in range(1, 4):
        next_round()
        a2a_p += exchange(proj, pk, PACK, peers[2 * distance : 2 * distance + 2])
        if distance == 1:
            a2a_g += exchange(gout, dk, OUT, peers[2:4])
    a2a_g += exchange(gout, dk, OUT, peers[4:])
    far_k, far_v = plan_relay(0), plan_relay(1)
    for near, far in ((near_k, far_k), (near_v, far_v)):
        for h in range(2):
            relay(h, near, far, fast)
    for h in range(2):
        relay(h, near_k, far_k, slow)
    sib_k += share_near(0)
    for h in range(2):
        relay(h, near_v, far_v, slow)
    sib_v += share_near(1)

    def spread(picked, window):
        for g in range(GROUP):
            part = picked[:, g * HEAD_DIM : (g + 1) * HEAD_DIM]
            window[:, g] = part.reshape(SEGS, SEG_MOST, HEAD_DIM)

    def gather_proj():
        own_proj.wait()
        for copy in a2a_p:
            copy.wait_recv()
        picked = dot(pick, pk[...].reshape(TOK_DEV, PACK), ((1,), (0,))).astype(BF16)
        spread(picked, win_q)
        for w in range(2):
            own = picked[:, OUT + w * HEAD_DIM : OUT + (w + 1) * HEAD_DIM].reshape(SEGS, SEG_MOST, HEAD_DIM)
            win_kv[w] = jnp.concatenate([own, jnp.zeros_like(own)], axis=1)

    def gather_gout():
        own_gout.wait()
        for copy in a2a_g:
            copy.wait_recv()
        spread(dot(pick, dk[...].reshape(TOK_DEV, OUT), ((1,), (0,))).astype(BF16), win_d)

    def all_rows(w, s):
        return jnp.concatenate([kv[w][slots[s]], win_kv[w, s]], axis=0)

    def queries(s):
        return win_q[s].reshape(STACK, HEAD_DIM)

    def dout(s):
        return win_d[s].reshape(STACK, HEAD_DIM)

    key_at = lax.broadcasted_iota(jnp.int32, (STACK, HEAD_DIM), 1)
    row_at = lax.rem(lax.broadcasted_iota(jnp.int32, (STACK, HEAD_DIM), 0), SEG_MOST)

    def weigh(s):
        scores = dot(queries(s), all_rows(0, s), ((1,), (1,)))
        own = jnp.where(key_at <= row_at, scores[:, PROMPT_LEN:], -1e30)
        scores = jnp.concatenate([scores[:, :PROMPT_LEN], own], axis=1)
        top = jnp.max(scores, axis=1, keepdims=True)
        expo = jnp.exp2((scores - top) * (SCALE * LOG2E))
        weights = expo * (1.0 / jnp.sum(expo, axis=1, keepdims=True))
        prob[s] = weights
        prob_b[s] = weights.astype(BF16)

    def value_terms(s):
        dvalue = dot(prob_b[s], dout(s), ((0,), (0,)))
        term[1, s] = dvalue[:PROMPT_LEN]
        win_g[s, GROUP + 1] = dvalue[PROMPT_LEN : PROMPT_LEN + SEG_MOST].astype(BF16)

    def attend(s):
        out = dot(prob_b[s], all_rows(1, s), ((1,), (0,))).astype(BF16)
        win_o[s] = out.reshape(GROUP, SEG_MOST, HEAD_DIM)

    def key_terms(s):
        out = win_o[s].reshape(STACK, HEAD_DIM)
        delta = jnp.sum(dout(s).astype(F32) * out.astype(F32), axis=1, keepdims=True)
        dweight = dot(dout(s), all_rows(1, s), ((1,), (1,)))
        dscore = (prob[s] * (dweight - delta) * SCALE).astype(BF16)
        dscore_b[s] = dscore
        dkey = dot(dscore, queries(s), ((0,), (0,)))
        term[0, s] = dkey[:PROMPT_LEN]
        win_g[s, GROUP] = dkey[PROMPT_LEN : PROMPT_LEN + SEG_MOST].astype(BF16)

    def query_terms(s):
        dquery = dot(dscore_b[s], all_rows(0, s), ((1,), (0,))).astype(BF16)
        win_g[s, :GROUP] = dquery.reshape(GROUP, SEG_MOST, HEAD_DIM)

    def summed(w, offset, part):
        total = jnp.zeros((part.size, HEAD_DIM), F32)
        for s in range(SEGS):
            total = total + jnp.where(offsets[s] == offset, term[w, s, part], 0.0)
        return total

    whole = pl.ds(0, PROMPT_LEN)

    def to_sibling(w):
        copies = [None] * 4
        for i, offset in ((3, 6 * core - 3), (0, -1 - 2 * core), (2, 3 - 2 * core), (1, 1 - 2 * core)):
            sib_send[w, i] = summed(w, offset, whole).astype(BF16)
            copies[i] = send(sib_send.at[w, i], sib_recv.at[w, i], sibling)
        return copies

    def to_far(w, sib):
        own = [[summed(w, 4, half), summed(w, -4, half)] for half in halves]
        sib[3].wait_recv()
        copies = []
        for (own_right, own_left), half in zip(own, halves):
            extra = sib_recv[w, 3, half].astype(F32)
            far_send[w, 0, half] = (own_right + jnp.where(core == 0, extra, 0.0)).astype(BF16)
            copies.append(send(far_send.at[w, 0, half], far_recv.at[w, 0, half], right))
            far_send[w, 1, half] = (own_left + jnp.where(core == 1, extra, 0.0)).astype(BF16)
            copies.append(send(far_send.at[w, 1, half], far_recv.at[w, 1, half], left))
        return copies

    def plan_near(w):
        copies = []
        for half in halves:
            copies += [prepare(near_send.at[w, i, half], near_recv.at[w, i, half], (right, left)[i]) for i in range(2)]
        return copies

    def to_near(w, h, sib, far, near, when):
        half = halves[h]
        for i in range(2):

            @pl.when(when[i])
            def _():
                part = summed(w, 2 - 4 * i, half) + sib_recv[w, 2 - 2 * i, half].astype(F32)
                far[2 * h + i].wait_recv()
                near_send[w, i, half] = (part + far_recv[w, i, half].astype(F32)).astype(BF16)
                near[2 * h + i].start()

    def finish(w, h, sib, near):
        half = halves[h]
        if h == 0:
            sib[1].wait_recv()
        total = summed(w, 0, half) + sib_recv[w, 1, half].astype(F32)
        for i in range(2):
            near[2 * h + i].wait_recv()
            total = total + near_recv[w, i, half].astype(F32)
        dcache_out[half, feature(w)] = total.astype(BF16)

    def give_back(window, staged, out, width, sem):
        parts = [window[:, g].reshape(SEGS * SEG_MOST, HEAD_DIM) for g in range(width // HEAD_DIM)]
        tokens = dot(unpick, jnp.concatenate(parts, axis=1), ((1,), (0,)))
        staged[...] = tokens.astype(BF16).reshape(N_HEAD, ROWS, width)
        copies = [send(staged.at[p], out.at[:, columns(head, width)], (dp, p)) for p in peers]
        own = pltpu.make_async_copy(staged.at[head], out.at[:, columns(head, width)], local_sem.at[sem])
        own.start()
        return copies, own

    sib_k += share_far(0, far_k)
    gather_proj()
    own_kv[0].wait()
    for copy in sib_k:
        copy.wait_recv()
    for s in range(SEGS):
        weigh(s)
    gather_gout()
    for s in range(SEGS):
        value_terms(s)
    value_sib = to_sibling(1)
    sib_v += share_far(1, far_v)
    value_far = to_far(1, value_sib)
    own_kv[1].wait()
    for copy in sib_v:
        copy.wait_recv()
    for s in range(SEGS):
        attend(s)
    for s in range(SEGS):
        key_terms(s)
    key_sib = to_sibling(0)
    att_copies, att_own = give_back(win_o, att_send, att_out, OUT, 0)
    value_near, key_near = plan_near(1), plan_near(0)
    value_sib[0].wait_recv()
    value_sib[2].wait_recv()
    to_near(1, 0, value_sib, value_far, value_near, fast)
    for s in range(SEGS):
        query_terms(s)
    grad_copies, grad_own = give_back(win_g, dproj_send, dproj_out, PACK, 1)
    key_far = to_far(0, key_sib)
    to_near(1, 1, value_sib, value_far, value_near, fast)
    for h in range(2):
        to_near(1, h, value_sib, value_far, value_near, slow)
    key_sib[0].wait_recv()
    key_sib[2].wait_recv()
    for when in (fast, slow):
        for h in range(2):
            to_near(0, h, key_sib, key_far, key_near, when)
    finish(1, 0, value_sib, value_near)
    finish(1, 1, value_sib, value_near)
    finish(0, 0, key_sib, key_near)
    finish(0, 1, key_sib, key_near)
    for copy in att_copies + grad_copies:
        copy.wait_recv()
    att_own.wait()
    grad_own.wait()
    assert len(sent) <= COPIES
    for copy in sent:
        copy.wait_send()


def hand_over(att, dproj, dcache, att_out, dproj_out, dcache_out, sems):
    copies = [
        pltpu.make_async_copy(src, dst, sems.at[i])
        for i, (src, dst) in enumerate(((att, att_out), (dproj, dproj_out), (dcache, dcache_out)))
    ]
    for copy in copies:
        copy.start()
    for copy in copies:
        copy.wait()


def local(projected, grad_output, prompt_cache, segment_ids, segment_prompt):
    hbm = pl.BlockSpec(memory_space=pltpu.HBM)
    vmem = pl.BlockSpec(memory_space=pltpu.VMEM)
    block = (PROMPT_LEN, HEAD_DIM)
    results = (
        jax.ShapeDtypeStruct(grad_output.shape, BF16),
        jax.ShapeDtypeStruct(projected.shape, BF16),
        jax.ShapeDtypeStruct(prompt_cache.shape, BF16),
    )
    outs = pl.pallas_call(
        kernel,
        out_shape=tuple(pltpu.VMEM(r.shape, BF16) for r in results),
        in_specs=[hbm] * 5,
        out_specs=(vmem, vmem, vmem),
        scratch_shapes=[
            pltpu.VMEM(segment_ids.shape, jnp.int32),
            pltpu.SMEM(segment_prompt.shape, jnp.int32),
            pltpu.VMEM((N_HEAD, ROWS, PACK), BF16),
            pltpu.VMEM((N_HEAD, ROWS, OUT), BF16),
            pltpu.VMEM((9,) + block, BF16),
            pltpu.VMEM((9,) + block, BF16),
            pltpu.VMEM((SEGS, GROUP, SEG_MOST, HEAD_DIM), BF16),
            pltpu.VMEM((2, SEGS, HEAD_DIM, HEAD_DIM), BF16),
            pltpu.VMEM((SEGS, GROUP, SEG_MOST, HEAD_DIM), BF16),
            pltpu.VMEM((SEGS, STACK, KEYS), F32),
            pltpu.VMEM((SEGS, STACK, KEYS), BF16),
            pltpu.VMEM((SEGS, STACK, KEYS), BF16),
            pltpu.VMEM((2, SEGS) + block, F32),
            pltpu.VMEM((SEGS, GROUP, SEG_MOST, HEAD_DIM), BF16),
            pltpu.VMEM((SEGS, GROUP + 2, SEG_MOST, HEAD_DIM), BF16),
            pltpu.VMEM((N_HEAD, ROWS, OUT), BF16),
            pltpu.VMEM((N_HEAD, ROWS, PACK), BF16),
            pltpu.VMEM((2, 4) + block, BF16),
            pltpu.VMEM((2, 4) + block, BF16),
            pltpu.VMEM((2, 2) + block, BF16),
            pltpu.VMEM((2, 2) + block, BF16),
            pltpu.VMEM((2, 2) + block, BF16),
            pltpu.VMEM((2, 2) + block, BF16),
            pltpu.SemaphoreType.DMA((6,)),
            pltpu.SemaphoreType.DMA((COPIES,)),
            pltpu.SemaphoreType.DMA((COPIES,)),
            pltpu.SemaphoreType.REGULAR((2,)),
        ],
        compiler_params=pltpu.CompilerParams(
            collective_id=0, has_side_effects=True, vmem_limit_bytes=60 << 20
        ),
    )(segment_ids, segment_prompt, projected, grad_output, prompt_cache)
    return pl.pallas_call(
        hand_over,
        out_shape=results,
        in_specs=[vmem] * 3,
        out_specs=(hbm,) * 3,
        scratch_shapes=[pltpu.SemaphoreType.DMA((3,))],
        compiler_params=pltpu.CompilerParams(vmem_limit_bytes=8 << 20),
    )(*outs)


def solution(mesh):
    return jax.shard_map(
        local,
        mesh=mesh,
        in_specs=(
            P(("dp", "head"), None),
            P(("dp", "head"), None),
            P("dp", "head"),
            P("dp", None),
            P("dp", None),
        ),
        out_specs=(P(("dp", "head"), None), P(("dp", "head"), None), P("dp", "head")),
        check_vma=False,
    )
```

```python
import jax
import jax.numpy as jnp
from jax import lax
from jax.experimental import pallas as pl
from jax.experimental.pallas import tpu as pltpu
from jax.sharding import PartitionSpec as P

HEADS = 40
KV_HEADS = 8
HEAD_DIM = 128
GROUP = HEADS // KV_HEADS
TOK_DEV = 128
PROMPT_LEN = 512
SEGS = 4
REACH = 4
SEG_MOST = 64
N_DP = 64
CHIPS = N_DP // 2
CHIPS_Z = 8
N_HEAD = 8
ROWS = TOK_DEV // N_HEAD
PACK = (GROUP + 2) * HEAD_DIM
OUT = GROUP * HEAD_DIM
STACK = GROUP * SEG_MOST
KEYS = PROMPT_LEN + HEAD_DIM
SCALE = HEAD_DIM**-0.5
LOG2E = 1.4426950408889634
MESH = pl.DeviceIdType.MESH
F32 = jnp.float32
BF16 = jnp.bfloat16
COPIES = 80
HALF = PROMPT_LEN // 2


def dot(left, right, contract):
    return lax.dot_general(left, right, (contract, ((), ())), preferred_element_type=F32)


def kernel(
    ids_hbm, owner_hbm, proj, gout, cache,
    att_out, dproj_out, dcache_out,
    ids_ref, owner_ref, pk, dk, keys, values, win_q, win_kv, win_d, prob, prob_b, dscore_b, term, win_o, win_g, att_send, dproj_send,
    sib_send, sib_recv, far_send, far_recv, near_send, near_recv,
    local_sem, send_sem, recv_sem, ring_sem,
):
    dp = lax.axis_index("dp")
    head = lax.axis_index("head")
    chip = dp // 2
    core = lax.rem(dp, 2)
    sibling = (dp + 1 - 2 * core, head)
    right = (lax.rem(chip + 1, CHIPS) * 2 + core, head)
    left = (lax.rem(chip + CHIPS - 1, CHIPS) * 2 + core, head)
    peers = [lax.rem(head + j, N_HEAD) for j in (1, 7, 2, 6, 3, 5, 4)]
    kv = (keys, values)
    sent = []

    def prepare(src, dst, device):
        i = len(sent)
        copy = pltpu.make_async_remote_copy(
            src_ref=src, dst_ref=dst, send_sem=send_sem.at[i], recv_sem=recv_sem.at[i],
            device_id=device, device_id_type=MESH,
        )
        sent.append(copy)
        return copy

    def send(src, dst, device):
        copy = prepare(src, dst, device)
        copy.start()
        return copy

    def columns(index, width):
        return pl.ds(pl.multiple_of(index * width, HEAD_DIM), width)

    def feature(w):
        return pl.ds(w * HEAD_DIM, HEAD_DIM)

    z = lax.rem(chip, CHIPS_Z)
    slow = (z == 0, z == CHIPS_Z - 1)
    fast = (z != 0, z != CHIPS_Z - 1)

    halves = [pl.ds(i * HALF, HALF) for i in range(2)]

    barrier = pltpu.get_barrier_semaphore()
    partners = [right, left, (dp, peers[0]), (dp, peers[1]), sibling]
    for partner in partners:
        pl.semaphore_signal(barrier, inc=1, device_id=partner, device_id_type=MESH)
    small = [
        pltpu.make_async_copy(ids_hbm, ids_ref, local_sem.at[4]),
        pltpu.make_async_copy(owner_hbm, owner_ref, local_sem.at[5]),
    ]
    own_kv = [pltpu.make_async_copy(cache.at[:, feature(w)], kv[w].at[2], local_sem.at[w]) for w in range(2)]
    own_proj = pltpu.make_async_copy(proj.at[:, columns(head, PACK)], pk.at[head], local_sem.at[2])
    own_gout = pltpu.make_async_copy(gout.at[:, columns(head, OUT)], dk.at[head], local_sem.at[3])
    for copy in small + own_kv + [own_proj, own_gout]:
        copy.start()
    for copy in small:
        copy.wait()

    ids = ids_ref[...]
    position = lax.broadcasted_iota(jnp.int32, (1, TOK_DEV), 1)
    first = jnp.zeros((1, TOK_DEV), jnp.int32)
    for s in range(SEGS):
        before = jnp.sum((ids < s).astype(jnp.int32), axis=1, keepdims=True)
        first = first + jnp.where(ids == s, before, 0)
    row = (ids * SEG_MOST + position - first).astype(F32)
    rows = lax.broadcasted_iota(jnp.int32, (SEGS * SEG_MOST, TOK_DEV), 0).astype(F32)
    pick = (jnp.broadcast_to(row, rows.shape) == rows).astype(BF16)
    row_t = jnp.transpose(jnp.broadcast_to(row, (TOK_DEV, TOK_DEV)))
    cols = lax.broadcasted_iota(jnp.int32, (TOK_DEV, SEGS * SEG_MOST), 1).astype(F32)
    unpick = (jnp.concatenate([row_t, row_t], axis=1) == cols).astype(BF16)

    offsets, slots = [], []
    for s in range(SEGS):
        offset = lax.rem(owner_ref[0, s] - dp + N_DP + REACH, N_DP) - REACH
        odd = lax.rem(offset + 8, 2)
        away = jnp.where(odd == 1, offset - 1 + 2 * core, offset) // 2
        slot = jnp.where(
            odd == 0, jnp.clip(away, -2, 2) + 2,
            jnp.where(away == 0, 5, jnp.where(away == 1, 6, jnp.where(away == -1, 7, 8))),
        )
        offsets.append(offset)
        slots.append(slot)

    pl.semaphore_wait(barrier, len(partners))

    def start_near(w):
        copies = []
        for half in halves:
            block = cache.at[half, feature(w)]
            copies.append(send(block, kv[w].at[1, half], right))
            copies.append(send(block, kv[w].at[3, half], left))
        return copies

    def plan_relay(w):
        copies = []
        for half in halves:
            copies.append(prepare(kv[w].at[1, half], kv[w].at[0, half], right))
            copies.append(prepare(kv[w].at[3, half], kv[w].at[4, half], left))
        return copies

    def relay(h, near, far, when):
        for side in range(2):

            @pl.when(when[side])
            def _():
                near[2 * h + side].wait_recv()
                far[2 * h + side].start()

    def share_near(w):
        return [send(kv[w].at[1], kv[w].at[7], sibling), send(kv[w].at[3], kv[w].at[6], sibling)]

    def share_far(w, far):
        for copy in far:
            copy.wait_recv()
        return [send(kv[w].at[4 - 4 * core], kv[w].at[8], sibling)]

    near_k = start_near(0)
    near_v = start_near(1)
    sib_k = [send(cache.at[:, feature(0)], keys.at[5], sibling)]
    sib_v = [send(cache.at[:, feature(1)], values.at[5], sibling)]

    def next_round():
        for i in range(2):
            pl.semaphore_signal(ring_sem.at[i], inc=1, device_id=(dp, peers[i]), device_id_type=MESH)
        for i in range(2):
            pl.semaphore_wait(ring_sem.at[i], 1)

    def exchange(block, staged, width, chosen):
        return [send(block.at[:, columns(p, width)], staged.at[head], (dp, p)) for p in chosen]

    a2a_p = exchange(proj, pk, PACK, peers[:2])
    a2a_g = exchange(gout, dk, OUT, peers[:2])
    for distance in range(1, 4):
        next_round()
        a2a_p += exchange(proj, pk, PACK, peers[2 * distance : 2 * distance + 2])
        a2a_g += exchange(gout, dk, OUT, peers[2 * distance : 2 * distance + 2])
    far_k, far_v = plan_relay(0), plan_relay(1)
    for near, far in ((near_k, far_k), (near_v, far_v)):
        for h in range(2):
            relay(h, near, far, fast)
    for h in range(2):
        relay(h, near_k, far_k, slow)
    sib_k += share_near(0)
    for h in range(2):
        relay(h, near_v, far_v, slow)
    sib_v += share_near(1)

    def spread(picked, window):
        for g in range(GROUP):
            part = picked[:, g * HEAD_DIM : (g + 1) * HEAD_DIM]
            window[:, g] = part.reshape(SEGS, SEG_MOST, HEAD_DIM)

    def gather_proj():
        own_proj.wait()
        for copy in a2a_p:
            copy.wait_recv()
        picked = dot(pick, pk[...].reshape(TOK_DEV, PACK), ((1,), (0,))).astype(BF16)
        spread(picked, win_q)
        for w in range(2):
            own = picked[:, OUT + w * HEAD_DIM : OUT + (w + 1) * HEAD_DIM].reshape(SEGS, SEG_MOST, HEAD_DIM)
            win_kv[w] = jnp.concatenate([own, jnp.zeros_like(own)], axis=1)

    def gather_gout():
        own_gout.wait()
        for copy in a2a_g:
            copy.wait_recv()
        spread(dot(pick, dk[...].reshape(TOK_DEV, OUT), ((1,), (0,))).astype(BF16), win_d)

    def all_rows(w, s):
        return jnp.concatenate([kv[w][slots[s]], win_kv[w, s]], axis=0)

    def queries(s):
        return win_q[s].reshape(STACK, HEAD_DIM)

    def dout(s):
        return win_d[s].reshape(STACK, HEAD_DIM)

    key_at = lax.broadcasted_iota(jnp.int32, (STACK, HEAD_DIM), 1)
    row_at = lax.rem(lax.broadcasted_iota(jnp.int32, (STACK, HEAD_DIM), 0), SEG_MOST)

    def weigh(s):
        scores = dot(queries(s), all_rows(0, s), ((1,), (1,)))
        own = jnp.where(key_at <= row_at, scores[:, PROMPT_LEN:], -1e30)
        scores = jnp.concatenate([scores[:, :PROMPT_LEN], own], axis=1)
        top = jnp.max(scores, axis=1, keepdims=True)
        expo = jnp.exp2((scores - top) * (SCALE * LOG2E))
        weights = expo * (1.0 / jnp.sum(expo, axis=1, keepdims=True))
        prob[s] = weights
        prob_b[s] = weights.astype(BF16)

    def value_terms(s):
        dvalue = dot(prob_b[s], dout(s), ((0,), (0,)))
        term[1, s] = dvalue[:PROMPT_LEN]
        win_g[s, GROUP + 1] = dvalue[PROMPT_LEN : PROMPT_LEN + SEG_MOST].astype(BF16)

    def attend(s):
        out = dot(prob_b[s], all_rows(1, s), ((1,), (0,))).astype(BF16)
        win_o[s] = out.reshape(GROUP, SEG_MOST, HEAD_DIM)

    def key_terms(s):
        out = win_o[s].reshape(STACK, HEAD_DIM)
        delta = jnp.sum(dout(s).astype(F32) * out.astype(F32), axis=1, keepdims=True)
        dweight = dot(dout(s), all_rows(1, s), ((1,), (1,)))
        dscore = (prob[s] * (dweight - delta) * SCALE).astype(BF16)
        dscore_b[s] = dscore
        dkey = dot(dscore, queries(s), ((0,), (0,)))
        term[0, s] = dkey[:PROMPT_LEN]
        win_g[s, GROUP] = dkey[PROMPT_LEN : PROMPT_LEN + SEG_MOST].astype(BF16)

    def query_terms(s):
        dquery = dot(dscore_b[s], all_rows(0, s), ((1,), (0,))).astype(BF16)
        win_g[s, :GROUP] = dquery.reshape(GROUP, SEG_MOST, HEAD_DIM)

    def summed(w, offset, part):
        total = jnp.zeros((part.size, HEAD_DIM), F32)
        for s in range(SEGS):
            total = total + jnp.where(offsets[s] == offset, term[w, s, part], 0.0)
        return total

    whole = pl.ds(0, PROMPT_LEN)

    def to_sibling(w):
        copies = [None] * 4
        for i, offset in ((3, 6 * core - 3), (0, -1 - 2 * core), (2, 3 - 2 * core), (1, 1 - 2 * core)):
            sib_send[w, i] = summed(w, offset, whole).astype(BF16)
            copies[i] = send(sib_send.at[w, i], sib_recv.at[w, i], sibling)
        return copies

    def to_far(w, sib):
        own = [[summed(w, 4, half), summed(w, -4, half)] for half in halves]
        sib[3].wait_recv()
        copies = []
        for (own_right, own_left), half in zip(own, halves):
            extra = sib_recv[w, 3, half].astype(F32)
            far_send[w, 0, half] = (own_right + jnp.where(core == 0, extra, 0.0)).astype(BF16)
            copies.append(send(far_send.at[w, 0, half], far_recv.at[w, 0, half], right))
            far_send[w, 1, half] = (own_left + jnp.where(core == 1, extra, 0.0)).astype(BF16)
            copies.append(send(far_send.at[w, 1, half], far_recv.at[w, 1, half], left))
        return copies

    def plan_near(w):
        copies = []
        for half in halves:
            copies += [prepare(near_send.at[w, i, half], near_recv.at[w, i, half], (right, left)[i]) for i in range(2)]
        return copies

    def to_near(w, h, sib, far, near, when):
        half = halves[h]
        for i in range(2):

            @pl.when(when[i])
            def _():
                part = summed(w, 2 - 4 * i, half) + sib_recv[w, 2 - 2 * i, half].astype(F32)
                far[2 * h + i].wait_recv()
                near_send[w, i, half] = (part + far_recv[w, i, half].astype(F32)).astype(BF16)
                near[2 * h + i].start()

    def finish(w, h, sib, near):
        half = halves[h]
        if h == 0:
            sib[1].wait_recv()
        total = summed(w, 0, half) + sib_recv[w, 1, half].astype(F32)
        for i in range(2):
            near[2 * h + i].wait_recv()
            total = total + near_recv[w, i, half].astype(F32)
        dcache_out[half, feature(w)] = total.astype(BF16)

    def give_back(window, staged, out, width, sem):
        parts = [window[:, g].reshape(SEGS * SEG_MOST, HEAD_DIM) for g in range(width // HEAD_DIM)]
        tokens = dot(unpick, jnp.concatenate(parts, axis=1), ((1,), (0,)))
        staged[...] = tokens.astype(BF16).reshape(N_HEAD, ROWS, width)
        copies = [send(staged.at[p], out.at[:, columns(head, width)], (dp, p)) for p in peers]
        own = pltpu.make_async_copy(staged.at[head], out.at[:, columns(head, width)], local_sem.at[sem])
        own.start()
        return copies, own

    sib_k += share_far(0, far_k)
    gather_proj()
    own_kv[0].wait()
    for copy in sib_k:
        copy.wait_recv()
    for s in range(SEGS):
        weigh(s)
    gather_gout()
    for s in range(SEGS):
        value_terms(s)
    value_sib = to_sibling(1)
    sib_v += share_far(1, far_v)
    value_far = to_far(1, value_sib)
    own_kv[1].wait()
    for copy in sib_v:
        copy.wait_recv()
    for s in range(SEGS):
        attend(s)
    for s in range(SEGS):
        key_terms(s)
    key_sib = to_sibling(0)
    att_copies, att_own = give_back(win_o, att_send, att_out, OUT, 0)
    value_near, key_near = plan_near(1), plan_near(0)
    value_sib[0].wait_recv()
    value_sib[2].wait_recv()
    to_near(1, 0, value_sib, value_far, value_near, fast)
    for s in range(SEGS):
        query_terms(s)
    grad_copies, grad_own = give_back(win_g, dproj_send, dproj_out, PACK, 1)
    key_far = to_far(0, key_sib)
    to_near(1, 1, value_sib, value_far, value_near, fast)
    for h in range(2):
        to_near(1, h, value_sib, value_far, value_near, slow)
    key_sib[0].wait_recv()
    key_sib[2].wait_recv()
    for when in (fast, slow):
        for h in range(2):
            to_near(0, h, key_sib, key_far, key_near, when)
    finish(1, 0, value_sib, value_near)
    finish(1, 1, value_sib, value_near)
    finish(0, 0, key_sib, key_near)
    finish(0, 1, key_sib, key_near)
    for copy in att_copies + grad_copies:
        copy.wait_recv()
    att_own.wait()
    grad_own.wait()
    assert len(sent) <= COPIES
    for copy in sent:
        copy.wait_send()


def hand_over(att, dproj, dcache, att_out, dproj_out, dcache_out, sems):
    copies = [
        pltpu.make_async_copy(src, dst, sems.at[i])
        for i, (src, dst) in enumerate(((att, att_out), (dproj, dproj_out), (dcache, dcache_out)))
    ]
    for copy in copies:
        copy.start()
    for copy in copies:
        copy.wait()


def local(projected, grad_output, prompt_cache, segment_ids, segment_prompt):
    hbm = pl.BlockSpec(memory_space=pltpu.HBM)
    vmem = pl.BlockSpec(memory_space=pltpu.VMEM)
    block = (PROMPT_LEN, HEAD_DIM)
    results = (
        jax.ShapeDtypeStruct(grad_output.shape, BF16),
        jax.ShapeDtypeStruct(projected.shape, BF16),
        jax.ShapeDtypeStruct(prompt_cache.shape, BF16),
    )
    outs = pl.pallas_call(
        kernel,
        out_shape=tuple(pltpu.VMEM(r.shape, BF16) for r in results),
        in_specs=[hbm] * 5,
        out_specs=(vmem, vmem, vmem),
        scratch_shapes=[
            pltpu.VMEM(segment_ids.shape, jnp.int32),
            pltpu.SMEM(segment_prompt.shape, jnp.int32),
            pltpu.VMEM((N_HEAD, ROWS, PACK), BF16),
            pltpu.VMEM((N_HEAD, ROWS, OUT), BF16),
            pltpu.VMEM((9,) + block, BF16),
            pltpu.VMEM((9,) + block, BF16),
            pltpu.VMEM((SEGS, GROUP, SEG_MOST, HEAD_DIM), BF16),
            pltpu.VMEM((2, SEGS, HEAD_DIM, HEAD_DIM), BF16),
            pltpu.VMEM((SEGS, GROUP, SEG_MOST, HEAD_DIM), BF16),
            pltpu.VMEM((SEGS, STACK, KEYS), F32),
            pltpu.VMEM((SEGS, STACK, KEYS), BF16),
            pltpu.VMEM((SEGS, STACK, KEYS), BF16),
            pltpu.VMEM((2, SEGS) + block, F32),
            pltpu.VMEM((SEGS, GROUP, SEG_MOST, HEAD_DIM), BF16),
            pltpu.VMEM((SEGS, GROUP + 2, SEG_MOST, HEAD_DIM), BF16),
            pltpu.VMEM((N_HEAD, ROWS, OUT), BF16),
            pltpu.VMEM((N_HEAD, ROWS, PACK), BF16),
            pltpu.VMEM((2, 4) + block, BF16),
            pltpu.VMEM((2, 4) + block, BF16),
            pltpu.VMEM((2, 2) + block, BF16),
            pltpu.VMEM((2, 2) + block, BF16),
            pltpu.VMEM((2, 2) + block, BF16),
            pltpu.VMEM((2, 2) + block, BF16),
            pltpu.SemaphoreType.DMA((6,)),
            pltpu.SemaphoreType.DMA((COPIES,)),
            pltpu.SemaphoreType.DMA((COPIES,)),
            pltpu.SemaphoreType.REGULAR((2,)),
        ],
        compiler_params=pltpu.CompilerParams(
            collective_id=0, has_side_effects=True, vmem_limit_bytes=60 << 20
        ),
    )(segment_ids, segment_prompt, projected, grad_output, prompt_cache)
    return pl.pallas_call(
        hand_over,
        out_shape=results,
        in_specs=[vmem] * 3,
        out_specs=(hbm,) * 3,
        scratch_shapes=[pltpu.SemaphoreType.DMA((3,))],
        compiler_params=pltpu.CompilerParams(vmem_limit_bytes=8 << 20),
    )(*outs)


def solution(mesh):
    return jax.shard_map(
        local,
        mesh=mesh,
        in_specs=(
            P(("dp", "head"), None),
            P(("dp", "head"), None),
            P("dp", "head"),
            P("dp", None),
            P("dp", None),
        ),
        out_specs=(P(("dp", "head"), None), P(("dp", "head"), None), P("dp", "head")),
        check_vma=False,
    )
```
